128 devices in a mesh: expert: 64 (over x, z, y), dp: 2 (over core).
Axes of the slice: x: 4, y: 4, z: 4, core: 2. Of those that a mesh axis runs over, the one named last changes fastest.
Arguments:
- tokens: bfloat16 [16384, 7168], P(('expert', 'dp')), may hold values from -6 to 6
- grad_out: bfloat16 [16384, 7168], P(('expert', 'dp')), may hold values from -6 to 6
- gates: float32 [16384, 8], P(('expert', 'dp')), may hold values from 0.1 to 0.6
- expert_ids: int32 [16384, 8], P(('expert', 'dp')), may hold values from 0 to 255, as said below
- expert_weights: bfloat16 [64, 192, 7168], P('expert', None, 'dp'), may hold values from -1 to 1
- moment_one: float32 [64, 192, 7168], P('expert', None, 'dp'), may hold values from -6 to 6
- moment_two: float32 [64, 192, 7168], P('expert', None, 'dp'), may hold values from 1 to 1000
Outputs:
- grad_tokens: bfloat16 [16384, 7168], P(('expert', 'dp'))
- new_moment_one: float32 [64, 192, 7168], P('expert', None, 'dp')
- new_moment_two: float32 [64, 192, 7168], P('expert', None, 'dp')
The draws below stay inside these ranges and needn't reach their ends.
Inputs may be any that keep to these rules, and one draw needn't show every extreme that they name: `expert_ids`: each row names 8 different experts. In each device's aligned block of 128 rows no expert under 4 is named by more than 8 rows; in every draw some expert under 4 is named by exactly 8 rows in every block.
All inputs are finite; a program needn't handle non-finite values.
Results may differ from the reference program's by a relative error of at most 0.0095.
Values may be sent and summed in bfloat16 or wider, within the bound.
No kernel may reach another device: no remote copies, remote signals or barrier semaphores. Data moves between devices by JAX's collectives and lax.ppermute only.
A program may use at most 128 MiB of HBM per device.

```python
import math
import jax
import jax.numpy as jnp
from jax import lax

D = 7168
SLAB = 1024
GROUP = 16
TOPK = 8
TOK_DEV = 128
HID = 64
EXPERTS = 4
ROUTED = 256
SLOT = 8
TOKENS = 16384
N_EXPERT = 64
N_DP = 2


def draw_expert_ids(key, part):
    key = jax.random.fold_in(key, 23)
    key_full, key_turn, key_count, key_member, key_outer = jax.random.split(key, 5)
    block_count = TOKENS // TOK_DEV
    full_expert = jax.random.randint(key_full, (), 0, EXPERTS)
    turn_start = jax.random.randint(key_turn, (), 0, EXPERTS)
    turning = (jnp.arange(block_count, dtype=jnp.int32) + turn_start) % EXPERTS
    window = jnp.arange(EXPERTS, dtype=jnp.int32)
    counts = jax.random.randint(key_count, (block_count, EXPERTS), 0, SLOT + 1)
    forced = (window[None, :] == full_expert) | (window[None, :] == turning[:, None])
    counts = jnp.where(forced, SLOT, counts)
    scores = jax.random.randint(key_member, (block_count, EXPERTS, TOK_DEV), 0, 4096) * TOK_DEV + jnp.arange(TOK_DEV, dtype=jnp.int32)
    ranks = jnp.argsort(jnp.argsort(scores, axis=2, stable=True), axis=2, stable=True).astype(jnp.int32)
    member = ranks < counts[:, :, None]
    member = jnp.transpose(member, (0, 2, 1)).reshape(TOKENS, EXPERTS)
    window_pick = jnp.where(member, window[None, :], ROUTED)
    outer_count = ROUTED - EXPERTS
    outer_scores = jax.random.randint(key_outer, (TOKENS, outer_count), 0, 4096) * outer_count + jnp.arange(outer_count, dtype=jnp.int32)
    outer_ids = lax.top_k(outer_scores, TOPK)[1].astype(jnp.int32) + EXPERTS
    joined = jnp.sort(jnp.concatenate([window_pick, outer_ids], axis=1), axis=1)
    return joined[:, :TOPK].astype(jnp.int32)


def draw_expert_weights(key, part):
    key = jax.random.fold_in(key, 11)
    key_left, key_right = jax.random.split(key)
    left = jnp.clip(jax.random.normal(key_left, (EXPERTS * GROUP, 2 * HID, D), jnp.float32), -4.0, 4.0) * D ** (-0.5)
    right = jnp.clip(jax.random.normal(key_right, (EXPERTS * GROUP, HID, D), jnp.float32), -4.0, 4.0) * SLAB ** (-0.5)
    joined = jnp.clip(jnp.concatenate([left, right], axis=1), -1.0, 1.0)
    return joined.astype(jnp.bfloat16)


def block_levels(key, extent, cuts, low, largest):
    level = 1.0
    for axis_at, blocks in cuts:
        heights = jax.random.uniform(jax.random.fold_in(jax.random.fold_in(key, 6), axis_at), (blocks,), jnp.float32, low / len(cuts), largest / len(cuts))
        level = level * jnp.repeat(jnp.exp(heights), extent[axis_at] // blocks).reshape((-1,) + (1,) * (len(extent) - 1 - axis_at))
    return level


def bell_draw(key, shape, width, bound, shards=(), kind=jnp.bfloat16):
    values = jax.random.normal(key, shape, jnp.float32) * width
    if len(shards) > 0:
        values = block_levels(key, shape, shards, -0.22, 0.18) * values
    return jnp.clip(values, min=-bound, max=bound).astype(kind)


def setup_inputs(seed: int = 0) -> dict:
    seeds = jax.random.split(jax.random.key(seed), 8)
    return {
        "tokens": bell_draw(seeds[0], (TOKENS, D), 1.0, 6.0, ((0, 128),)),
        "grad_out": bell_draw(seeds[1], (TOKENS, D), 1.0, 6.0, ((0, 128),)),
        "gates": jnp.clip(0.1 + 0.5 * jax.random.uniform(seeds[2], (TOKENS, TOPK), jnp.float32) ** block_levels(seeds[2], (TOKENS, TOPK), ((0, 128),), -0.2, 0.2), 0.1, 0.6),
        "expert_ids": draw_expert_ids(jax.random.fold_in(seeds[7], 71), 0),
        "expert_weights": draw_expert_weights(jax.random.fold_in(seeds[7], 71), 0),
        "moment_one": bell_draw(seeds[5], (EXPERTS * GROUP, 3 * HID, D), 1.0, 6.0, ((0, 64), (2, 2)), jnp.float32),
        "moment_two": jnp.clip(jnp.exp(math.log(1000.0) - 6.9077553 * jax.random.uniform(seeds[6], (EXPERTS * GROUP, 3 * HID, D), jnp.float32) ** block_levels(seeds[6], (EXPERTS * GROUP, 3 * HID, D), ((0, 64), (2, 2)), -0.2, 0.2)), 1.0, 1000.0),
    }


beta_one = 0.9
beta_two = 0.95


def block_rows(inputs, grads, weights):
    slab_width = weights.shape[0] // 3
    w_pair = weights[:2 * slab_width]
    w_down = weights[2 * slab_width:]
    pair_pre = lax.dot_general(inputs, w_pair, (((1,), (1,)), ((), ())), preferred_element_type=jnp.float32)
    gate_pre = pair_pre[:, :slab_width]
    up_pre = pair_pre[:, slab_width:]
    sigmoid_gate = jax.nn.sigmoid(gate_pre)
    activated = gate_pre * sigmoid_gate
    hidden = (activated * up_pre).astype(jnp.bfloat16)
    d_hidden = lax.dot_general(grads, w_down, (((1,), (1,)), ((), ())), preferred_element_type=jnp.float32)
    d_gate = d_hidden * up_pre * sigmoid_gate * (1.0 + gate_pre * (1.0 - sigmoid_gate))
    d_up = d_hidden * activated
    d_pair = jnp.concatenate([d_gate, d_up], axis=1).astype(jnp.bfloat16)
    back_rows = jnp.dot(d_pair, w_pair, preferred_element_type=jnp.float32).astype(jnp.bfloat16)
    in_terms = lax.dot_general(d_pair, inputs, (((0,), (0,)), ((), ())), preferred_element_type=jnp.float32)
    out_terms = lax.dot_general(hidden, grads, (((0,), (0,)), ((), ())), preferred_element_type=jnp.float32)
    return back_rows, jnp.concatenate([in_terms, out_terms], axis=0)


def adamw_moments(weight_grad, moment_a, moment_b):
    new_a = beta_one * moment_a + (1.0 - beta_one) * weight_grad
    new_b = beta_two * moment_b + (1.0 - beta_two) * weight_grad * weight_grad
    return new_a, new_b


def reference(tokens, grad_out, gates, expert_ids, expert_weights, moment_one, moment_two):
    flat_ids = expert_ids.reshape(-1).astype(jnp.int32)
    rows_all = flat_ids.shape[0]
    capacity = N_EXPERT * N_DP * SLOT
    in_window = flat_ids < EXPERTS
    onehot = (flat_ids[:, None] == jnp.arange(EXPERTS, dtype=jnp.int32)[None, :]).astype(jnp.int32)
    before = jnp.cumsum(onehot, axis=0, dtype=jnp.int32) - onehot
    position = jnp.sum(before * onehot, axis=1, dtype=jnp.int32)
    table_row = jnp.where(in_window, flat_ids, EXPERTS).astype(jnp.int32)
    fill_table = jnp.zeros((EXPERTS + 1, capacity), jnp.int32).at[table_row, position].set(jnp.arange(rows_all, dtype=jnp.int32) + 1)
    fill_table = fill_table[:EXPERTS]
    flat_gates = gates.reshape(-1)
    weights_all = expert_weights.reshape(EXPERTS, GROUP, 3 * HID, D)
    first_all = moment_one.reshape(EXPERTS, GROUP, 3 * HID, D)
    second_all = moment_two.reshape(EXPERTS, GROUP, 3 * HID, D)

    def per_expert(running, pieces):
        fill_row, weights_e, moment_a, moment_b = pieces
        occupied = fill_row > 0
        source_row = jnp.maximum(fill_row - 1, 0).astype(jnp.int32)
        source_tok = (source_row // TOPK).astype(jnp.int32)
        slot_gate = jnp.where(occupied, flat_gates[source_row], jnp.zeros((), flat_gates.dtype))
        inputs = jnp.where(occupied[:, None], tokens[source_tok], jnp.zeros((), tokens.dtype))
        grads = (slot_gate[:, None] * grad_out[source_tok].astype(slot_gate.dtype)).astype(jnp.bfloat16)

        def per_block(accum, block_pieces):
            weights, first, second = block_pieces
            back_rows, weight_grad = block_rows(inputs, grads, weights)
            accum = accum + back_rows.astype(accum.dtype)
            return accum, adamw_moments(weight_grad, first, second)

        start_acc = jnp.zeros((capacity, D), jnp.float32)
        accum, (new_a, new_b) = lax.scan(per_block, start_acc, (weights_e, moment_a, moment_b))
        added = jnp.where(occupied[:, None], accum.astype(running.dtype), jnp.zeros((), running.dtype))
        running = running.at[source_tok].add(added)
        return running, (new_a, new_b)

    start = jnp.zeros((TOKENS, D), jnp.float32)
    total, (new_a, new_b) = lax.scan(per_expert, start, (fill_table, weights_all, first_all, second_all))
    new_a = new_a.reshape(EXPERTS * GROUP, 3 * HID, D)
    new_b = new_b.reshape(EXPERTS * GROUP, 3 * HID, D)
    return total.astype(jnp.bfloat16), new_a, new_b
```

```python
import functools

import jax
import jax.numpy as jnp
from jax import lax
from jax.experimental import pallas as pl
from jax.experimental.pallas import tpu as pltpu
from jax.sharding import PartitionSpec as P

N = 4
SLOT = 8
HID = 64
D = 7168
HALF = D // 2
EIGHTH = HALF // N
QUARTER = 2 * EIGHTH
ROWS = N * SLOT
GROUPED = N * ROWS
BF = jnp.bfloat16
F32 = jnp.float32
beta_one = 0.9
beta_two = 0.95


def rotation(axis, step):
    pairs = []
    for x in range(N):
        for z in range(N):
            for y in range(N):
                for c in range(2):
                    to = {"x": x, "z": z, "y": y, "c": c}
                    to[axis] = (to[axis] + step) % (2 if axis == "c" else N)
                    source = ((x * N + z) * N + y) * 2 + c
                    target = ((to["x"] * N + to["z"]) * N + to["y"]) * 2 + to["c"]
                    pairs.append((source, target))
    return pairs


def turn(value, axis, step):
    return lax.ppermute(value, ("expert", "dp"), rotation(axis, step))


def call(kernel, name, outs, place, *ins, flops=0, scratch=()):
    outs = [jax.ShapeDtypeStruct(s, t) for s, t in outs]
    size = sum(v.size * v.dtype.itemsize for v in (*ins, *outs))
    return pl.pallas_call(
        kernel,
        name=name,
        out_shape=outs,
        in_specs=[pl.BlockSpec(memory_space=pltpu.SMEM)]
        + [pl.BlockSpec(memory_space=pltpu.VMEM)] * len(ins),
        out_specs=[pl.BlockSpec(memory_space=pltpu.VMEM)] * len(outs),
        scratch_shapes=list(scratch),
        cost_estimate=pl.CostEstimate(flops=flops, bytes_accessed=size, transcendentals=0),
        compiler_params=pltpu.CompilerParams(vmem_limit_bytes=32 * 1024 * 1024),
    )(place, *ins)


def wrap(v):
    return lax.rem(v + 2 * N, N)


def aligned(v):
    return pl.multiple_of(v, 128)


def mm(a, b, dims):
    return lax.dot_general(a, b, (dims, ((), ())), preferred_element_type=F32)


NN = ((1,), (0,))
NT = ((1,), (1,))
TN = ((0,), (0,))


def route_kernel(place, ids, gates, tokens, o0, o1, o2, o3, pick_out, pick_t_out, gate_out):
    tok = ids.shape[0]
    x = place[0]
    idv = ids[...]
    gv = gates[...]
    lane = lax.broadcasted_iota(jnp.int32, (tok, 128), 1)
    masks = jnp.zeros((tok, 128), F32)
    columns = []
    for k in range(N):
        hit = idv == wrap(x + k)
        member = jnp.sum(hit.astype(F32), axis=1, keepdims=True)
        gate = jnp.sum(jnp.where(hit, gv, 0.0), axis=1, keepdims=True)
        masks = jnp.where(lane == k, member, masks)
        columns.append((member, gate))
    row_i = lax.broadcasted_iota(jnp.int32, (tok, tok), 0)
    col_i = lax.broadcasted_iota(jnp.int32, (tok, tok), 1)
    earlier = (col_i < row_i).astype(BF)
    before = mm(earlier, masks.astype(BF), NN)
    pick = jnp.zeros((tok, 128), F32)
    weighted = jnp.zeros((tok, 128), F32)
    for k in range(N):
        member, gate = columns[k]
        spot = before[:, k : k + 1].astype(jnp.int32) + k * SLOT
        on = (lane == spot) & (member > 0.0)
        pick = jnp.where(on, 1.0, pick)
        weighted = jnp.where(on, gate, weighted)
    pick_t = jnp.transpose(pick)[:ROWS]
    gate_out[...] = jnp.sum(jnp.transpose(weighted)[:ROWS], axis=1, keepdims=True)
    pick_out[...] = pick[:, :ROWS].astype(BF)
    pick_t = pick_t.astype(BF)
    pick_t_out[...] = pick_t
    for q in range(N):
        cols = slice(q * QUARTER, (q + 1) * QUARTER)
        got = mm(pick_t, tokens[:, cols], NN)
        for k, o in enumerate((o0, o1, o2, o3)):
            o[:, cols] = got[k * SLOT : (k + 1) * SLOT].astype(BF)


def grads_kernel(place, pick_t, gate, grad_out, o0, o1, o2, o3):
    for q in range(N):
        cols = slice(q * QUARTER, (q + 1) * QUARTER)
        got = mm(pick_t[...], grad_out[:, cols], NN) * gate[...]
        for k, o in enumerate((o0, o1, o2, o3)):
            o[:, cols] = got[k * SLOT : (k + 1) * SLOT].astype(BF)


def split_kernel(place, i0, i1, i2, i3, o0, o1, o2, o3):
    y = place[2]
    for k, o in enumerate((o0, o1, o2, o3)):
        q = wrap(y + k)
        for c in range(2):
            cols = pl.ds(aligned(c * HALF + q * EIGHTH), EIGHTH)
            rows = jnp.concatenate([r[:, cols].astype(F32) for r in (i0, i1, i2, i3)], axis=0)
            o[:, c * EIGHTH : (c + 1) * EIGHTH] = rows.astype(BF)


def pair_kernel(place, i0, i1, i2, i3, a, b):
    a[:ROWS] = i0[...]
    a[ROWS:] = i1[...]
    b[:ROWS] = i2[...]
    b[ROWS:] = i3[...]


def stack_weights_kernel(place, w0, w1, w2, w3, out):
    y = place[2]
    for k, w in enumerate((w0, w1, w2, w3)):
        block = wrap(y - k)
        for part in range(3):
            rows = pl.ds(pl.multiple_of(part * N * HID + block * HID, HID), HID)
            out[rows, :] = w[part * HID : (part + 1) * HID]


def split_columns_kernel(place, w, o0, o1, o2, o3):
    y = place[2]
    for k, o in enumerate((o0, o1, o2, o3)):
        o[...] = w[0, :, pl.ds(aligned(wrap(y + k) * EIGHTH), EIGHTH)]


def forward_kernel(lo, hi, place, a0, b0, a1, b1, a2, b2, a3, b3, own, other, o0, o1, o2, o3):
    c = place[3]
    mine = pl.ds(aligned(c * EIGHTH), EIGHTH)
    theirs = pl.ds(aligned((1 - c) * EIGHTH), EIGHTH)
    w_own = own[lo:hi]
    w_other = other[lo:hi]
    for n, (a, b) in enumerate(((a0, b0), (a1, b1), (a2, b2), (a3, b3))):
        for h, v in enumerate((a, b)):
            part = mm(v[:, mine], w_own, NT) + mm(v[:, theirs], w_other, NT)
            for s in range(2):
                o = (o0, o1, o2, o3)[2 * h + s]
                o[n * ROWS : (n + 1) * ROWS] = part[s * ROWS : (s + 1) * ROWS].astype(o.dtype)


def middle_kernel(place, p0, p1, p2, p3, d0, d1, d2, d3, out):
    width = N * HID
    pair = p0[...] + p1[...].astype(F32) + p2[...].astype(F32) + p3[...].astype(F32)
    d_hidden = d0[...] + d1[...].astype(F32) + d2[...].astype(F32) + d3[...].astype(F32)
    gate = pair[:, :width]
    up = pair[:, width:]
    sig = jax.nn.sigmoid(gate)
    act = gate * sig
    out[:, :width] = (d_hidden * up * sig * (1.0 + gate * (1.0 - sig))).astype(BF)
    out[:, width : 2 * width] = (d_hidden * act).astype(BF)
    out[:, 2 * width :] = (act * up).astype(BF)


def back_kernel(place, h0, h1, h2, h3, own, other, o0, o1, o2, o3):
    c = place[3]
    width = 2 * N * HID
    for n, o in enumerate((o0, o1, o2, o3)):
        rows = slice(n * ROWS, (n + 1) * ROWS)
        h = jnp.concatenate([r[rows, :width] for r in (h0, h1, h2, h3)], axis=0)
        o[:, pl.ds(aligned(c * EIGHTH), EIGHTH)] = mm(h, own[:width], NN).astype(BF)
        o[:, pl.ds(aligned((1 - c) * EIGHTH), EIGHTH)] = mm(h, other[:width], NN).astype(BF)


def weight_grad_kernel(place, h0, h1, h2, h3, *refs):
    xs, gs, (mine, theirs) = refs[:8], refs[8:16], refs[16:]
    c = place[3]
    width = 2 * N * HID
    hs = jnp.concatenate(
        [r[n * ROWS : (n + 1) * ROWS] for n in range(N) for r in (h0, h1, h2, h3)], axis=0
    )
    for o, half in ((theirs, 1 - c), (mine, c)):
        cols = pl.ds(aligned(half * EIGHTH), EIGHTH)
        x = jnp.concatenate([v[:, cols] for v in xs], axis=0)
        o[:width] = mm(hs[:, :width], x, TN).astype(o.dtype)
        g = jnp.concatenate([v[:, cols] for v in gs], axis=0)
        o[width:] = mm(hs[:, width:], g, TN).astype(o.dtype)


def grad_blocks_kernel(place, mine, got, o0, o1, o2, o3):
    y = place[2]
    for k, o in enumerate((o0, o1, o2, o3)):
        block = wrap(y - k)
        for part in range(3):
            rows = pl.ds(pl.multiple_of(part * N * HID + block * HID, HID), HID)
            total = mine[rows, :] + got[rows, :].astype(F32)
            o[part * HID : (part + 1) * HID] = total.astype(o.dtype)


def sum_back_kernel(place, r0, r1, r2, r3, o0, o1, o2, o3):
    for m, o in enumerate((o0, o1, o2, o3)):
        rows = slice(m * ROWS, (m + 1) * ROWS)
        total = (r0[rows].astype(F32) + r1[rows].astype(F32)) + (
            r2[rows].astype(F32) + r3[rows].astype(F32)
        )
        o[...] = total.astype(BF)


def join_kernel(place, i0, i1, i2, i3, o0, o1, o2, o3):
    y = place[2]
    for m, v in enumerate((i0, i1, i2, i3)):
        q = wrap(y + m)
        for c in range(2):
            cols = pl.ds(aligned(c * HALF + q * EIGHTH), EIGHTH)
            value = v[:, c * EIGHTH : (c + 1) * EIGHTH].astype(F32)
            for p, o in enumerate((o0, o1, o2, o3)):
                o[:, cols] = value[p * SLOT : (p + 1) * SLOT].astype(BF)


def combine_kernel(place, pick, r0, r1, r2, r3, out):
    for q in range(N):
        cols = slice(q * QUARTER, (q + 1) * QUARTER)
        rows = jnp.concatenate([r[:, cols].astype(F32) for r in (r0, r1, r2, r3)], axis=0)
        out[:, cols] = mm(pick[...], rows.astype(BF), NN).astype(BF)


def moments_kernel(place, g0, g1, g2, g3, one, two, new_one, new_two):
    step = pl.program_id(0)
    for k, g in enumerate((g0, g1, g2, g3)):

        @pl.when(step == k)
        def _():
            grad = g[...].astype(F32)
            new_one[0] = beta_one * one[0] + (1.0 - beta_one) * grad
            new_two[0] = beta_two * two[0] + (1.0 - beta_two) * grad * grad


def moments(place, grads, one, two):
    rows = one.shape[1]
    piece = pl.BlockSpec((rows, EIGHTH), lambda k, place: (0, 0))
    block = pl.BlockSpec((1, rows, EIGHTH), lambda k, place: (0, 0, lax.rem(place[2] + k, N)))
    return pl.pallas_call(
        moments_kernel,
        name="moments",
        grid_spec=pltpu.PrefetchScalarGridSpec(
            num_scalar_prefetch=1,
            grid=(N,),
            in_specs=[piece] * N + [block] * 2,
            out_specs=[block] * 2,
        ),
        out_shape=[jax.ShapeDtypeStruct(v.shape, v.dtype) for v in (one, two)],
        cost_estimate=pl.CostEstimate(
            flops=6 * one.size, bytes_accessed=17 * one.size, transcendentals=0
        ),
        compiler_params=pltpu.CompilerParams(vmem_limit_bytes=32 * 1024 * 1024),
    )(place, *grads, one, two)


def spread(parts, axis, sign=1):
    return [parts[0]] + [turn(parts[k], axis, sign * k) for k in range(1, N)]


def ring_gather(place, parts):
    a0, b0 = call(pair_kernel, "pair", [((2 * ROWS, QUARTER), BF)] * 2, place, *parts)
    a1, b1 = turn(a0, "z", 1), turn(b0, "z", 1)
    a3, b3 = turn(a0, "z", -1), turn(b0, "z", -1)
    a2 = turn(a1, "z", 1)
    b2 = turn(b3, "z", -1)
    return [a0, b0, a1, b1, a2, b2, a3, b3]


def shards(tokens, grad_out, gates, expert_ids, expert_weights, moment_one, moment_two):
    expert = lax.axis_index("expert")
    core = lax.axis_index("dp")
    place = jnp.stack([expert // (N * N), expert // N % N, expert % N, core]).astype(jnp.int32)
    tok = tokens.shape[0]
    width = N * HID
    slot_out = [((SLOT, D), BF)] * N
    row_out = [((ROWS, QUARTER), BF)] * N
    block_rows = expert_weights.shape[1]

    *inputs, pick, pick_t, gate = call(
        route_kernel,
        "route",
        slot_out + [((tok, ROWS), BF), ((ROWS, tok), BF), ((ROWS, 1), F32)],
        place,
        expert_ids,
        gates,
        tokens,
        flops=2 * ROWS * tok * D,
    )
    inputs = spread(inputs, "x")
    grads = call(
        grads_kernel, "grads", slot_out, place, pick_t, gate, grad_out, flops=2 * ROWS * tok * D
    )
    grads = spread(grads, "x")
    w_parts = call(
        split_columns_kernel,
        "split_columns",
        [((block_rows, EIGHTH), BF)] * N,
        place,
        expert_weights,
    )
    inputs = spread(call(split_kernel, "split", row_out, place, *inputs), "y")
    grads = spread(call(split_kernel, "split", row_out, place, *grads), "y")
    w_parts = spread(w_parts, "y")
    (w_own,) = call(
        stack_weights_kernel, "stack_weights", [((N * block_rows, EIGHTH), BF)], place, *w_parts
    )
    w_other = turn(w_own, "c", 1)
    inputs = ring_gather(place, inputs)
    grads = ring_gather(place, grads)

    pair = call(
        functools.partial(forward_kernel, 0, 2 * width),
        "pair_part",
        [((GROUPED, 2 * width), F32)] + [((GROUPED, 2 * width), BF)] * 3,
        place,
        *inputs,
        w_own,
        w_other,
        flops=2 * N * GROUPED * QUARTER * 2 * width,
    )
    pair = spread(pair, "y", -1)
    d_hidden = call(
        functools.partial(forward_kernel, 2 * width, 3 * width),
        "d_hidden_part",
        [((GROUPED, width), F32)] + [((GROUPED, width), BF)] * 3,
        place,
        *grads,
        w_own,
        w_other,
        flops=2 * N * GROUPED * QUARTER * width,
    )
    d_hidden = spread(d_hidden, "y", -1)
    (held,) = call(
        middle_kernel, "middle", [((GROUPED, 3 * width), BF)], place, *pair, *d_hidden
    )
    held = [held] + [turn(held, "y", k) for k in range(1, N)]

    back = call(
        back_kernel,
        "back",
        [((GROUPED, QUARTER), BF)] * N,
        place,
        *held,
        w_own,
        w_other,
        flops=2 * N * GROUPED * QUARTER * 2 * width,
    )
    back = spread(back, "z", -1)
    grad_mine, grad_theirs = call(
        weight_grad_kernel,
        "weight_grad",
        [((3 * width, EIGHTH), F32), ((3 * width, EIGHTH), BF)],
        place,
        *held,
        *inputs,
        *grads,
        flops=2 * N * GROUPED * QUARTER * 3 * width,
    )
    grad_got = turn(grad_theirs, "c", 1)
    blocks = call(
        grad_blocks_kernel,
        "grad_blocks",
        [((block_rows, EIGHTH), F32)] + [((block_rows, EIGHTH), BF)] * 3,
        place,
        grad_mine,
        grad_got,
    )
    back = spread(call(sum_back_kernel, "sum_back", row_out, place, *back), "y", -1)
    blocks = spread(blocks, "y", -1)
    back = spread(call(join_kernel, "join", slot_out, place, *back), "x", -1)
    new_one, new_two = moments(place, blocks, moment_one, moment_two)
    (grad_tokens,) = call(
        combine_kernel,
        "combine",
        [((tok, D), BF)],
        place,
        pick,
        *back,
        flops=2 * ROWS * tok * D,
    )
    return grad_tokens, new_one, new_two


def solution(mesh):
    return jax.shard_map(
        shards,
        mesh=mesh,
        in_specs=(
            P(("expert", "dp"), None),
            P(("expert", "dp"), None),
            P(("expert", "dp"), None),
            P(("expert", "dp"), None),
            P("expert", None, "dp"),
            P("expert", None, "dp"),
            P("expert", None, "dp"),
        ),
        out_specs=(P(("expert", "dp"), None), P("expert", None, "dp"), P("expert", None, "dp")),
        check_vma=False,
    )
```

```python
import functools

import jax
import jax.numpy as jnp
from jax import lax
from jax.experimental import pallas as pl
from jax.experimental.pallas import tpu as pltpu
from jax.sharding import PartitionSpec as P

N = 4
SLOT = 8
HID = 64
D = 7168
HALF = D // 2
EIGHTH = HALF // N
QUARTER = 2 * EIGHTH
ROWS = N * SLOT
GROUPED = N * ROWS
HELD = 2 * ROWS
CHUNK = N * HELD
BF = jnp.bfloat16
F32 = jnp.float32
VMEM_LIMIT = 16 * 1024 * 1024
VMEM_MOST = 56 * 1024 * 1024
beta_one = 0.9
beta_two = 0.95


def rotation(axis, step):
    pairs = []
    for x in range(N):
        for z in range(N):
            for y in range(N):
                for c in range(2):
                    to = {"x": x, "z": z, "y": y, "c": c}
                    to[axis] = (to[axis] + step) % (2 if axis == "c" else N)
                    source = ((x * N + z) * N + y) * 2 + c
                    target = ((to["x"] * N + to["z"]) * N + to["y"]) * 2 + to["c"]
                    pairs.append((source, target))
    return pairs


def turn(value, axis, step):
    return lax.ppermute(value, ("expert", "dp"), rotation(axis, step))


def call(kernel, name, outs, place, *ins, flops=0, scratch=()):
    outs = [jax.ShapeDtypeStruct(s, t) for s, t in outs]
    size = sum(v.size * v.dtype.itemsize for v in (*ins, *outs))
    return pl.pallas_call(
        kernel,
        name=name,
        out_shape=outs,
        in_specs=[pl.BlockSpec(memory_space=pltpu.SMEM)]
        + [pl.BlockSpec(memory_space=pltpu.VMEM)] * len(ins),
        out_specs=[pl.BlockSpec(memory_space=pltpu.VMEM)] * len(outs),
        scratch_shapes=list(scratch),
        cost_estimate=pl.CostEstimate(flops=flops, bytes_accessed=size, transcendentals=0),
        compiler_params=pltpu.CompilerParams(vmem_limit_bytes=VMEM_LIMIT),
    )(place, *ins)


def wrap(v):
    return lax.rem(v + 2 * N, N)


def aligned(v):
    return pl.multiple_of(v, 128)


def mm(a, b, dims):
    return lax.dot_general(a, b, (dims, ((), ())), preferred_element_type=F32)


NN = ((1,), (0,))
NT = ((1,), (1,))
TN = ((0,), (0,))


def route_kernel(
    ids_in, gates_in, tokens, grads, out, pick_out, ids, gates, tok_buf, grad_buf, sems
):
    tok = ids.shape[1]
    small = [
        pltpu.make_async_copy(ids_in, ids, sems.at[4 * N]),
        pltpu.make_async_copy(gates_in, gates, sems.at[4 * N + 1]),
    ]
    for copy in small:
        copy.start()
    copies = []
    for q in range(N):
        for i, (source, buf) in enumerate(((tokens, tok_buf), (grads, grad_buf))):
            for c in range(2):
                cols = pl.ds(c * HALF + q * EIGHTH, EIGHTH)
                copy = pltpu.make_async_copy(
                    source.at[:, cols], buf.at[:, cols], sems.at[q * 4 + i * 2 + c]
                )
                copy.start()
                copies.append(copy)
    row_i = lax.broadcasted_iota(jnp.int32, (tok, tok), 0)
    col_i = lax.broadcasted_iota(jnp.int32, (tok, tok), 1)
    slot = lax.broadcasted_iota(jnp.int32, (ROWS, tok), 0)
    for copy in small:
        copy.wait()
    idv = ids[...]
    gv = gates[...]
    hits = [idv == e for e in range(N)]
    members = [jnp.sum(h.astype(F32), axis=0, keepdims=True) for h in hits]
    chosen = [jnp.sum(jnp.where(h, gv, 0.0), axis=0, keepdims=True) for h in hits]
    mask = jnp.concatenate(members + [jnp.zeros((8 - N, tok), F32)], axis=0)
    before = mm(mask, (row_i < col_i).astype(F32), NN).astype(jnp.int32)
    place_of = jnp.zeros((ROWS, tok), jnp.int32)
    weight = jnp.zeros((ROWS, tok), F32)
    for e in range(N):
        spot = jnp.where(members[e] > 0.0, before[e : e + 1] + e * SLOT, -1)
        mine = slot // SLOT == e
        place_of = jnp.where(mine, spot, place_of)
        weight = jnp.where(mine, chosen[e], weight)
    on = place_of == slot
    pick = jnp.where(on, 1.0, 0.0).astype(BF)
    pick_out[...] = pick
    gate = jnp.sum(jnp.where(on, weight, 0.0), axis=1, keepdims=True)
    for q in range(N):
        for copy in copies[q * 4 : q * 4 + 4]:
            copy.wait()
        for c in range(2):
            cols = slice(c * HALF + q * EIGHTH, c * HALF + (q + 1) * EIGHTH)
            rows = mm(pick, tok_buf[:, cols], NN)
            scaled = mm(pick, grad_buf[:, cols], NN) * gate
            for e in range(N):
                at = slice(e * SLOT, (e + 1) * SLOT)
                both = jnp.concatenate([rows[at], scaled[at]], axis=0).astype(BF)
                out[e * N + q, :, c * EIGHTH : (c + 1) * EIGHTH] = both


def route(ids, gates, tokens, grad_out):
    tok = tokens.shape[0]
    vmem = pl.BlockSpec(memory_space=pltpu.VMEM)
    hbm = pl.BlockSpec(memory_space=pltpu.HBM)
    return pl.pallas_call(
        route_kernel,
        name="route",
        in_specs=[hbm] * 4,
        out_specs=[vmem, vmem],
        out_shape=[
            jax.ShapeDtypeStruct((N * N, 2 * SLOT, QUARTER), BF),
            jax.ShapeDtypeStruct((ROWS, tok), BF),
        ],
        scratch_shapes=[
            pltpu.VMEM(ids.shape, jnp.int32),
            pltpu.VMEM(gates.shape, F32),
            pltpu.VMEM((tok, D), BF),
            pltpu.VMEM((tok, D), BF),
            pltpu.SemaphoreType.DMA((4 * N + 2,)),
        ],
        cost_estimate=pl.CostEstimate(
            flops=4 * ROWS * tok * D, bytes_accessed=6 * tok * D, transcendentals=0
        ),
        compiler_params=pltpu.CompilerParams(vmem_limit_bytes=VMEM_MOST),
    )(ids, gates, tokens, grad_out)


def pair_kernel(place, got, a, b):
    for g in range(N):
        pieces = [got[x * N + g].astype(F32) for x in range(N)]
        for part in range(2):
            rows = [v[part * SLOT : (part + 1) * SLOT] for v in pieces]
            at = (part * 2 + g % 2) * ROWS
            (a, b)[g // 2][at : at + ROWS] = jnp.concatenate(rows, axis=0).astype(BF)


def stack_kernel(place, a0, b0, a1, b3, plus, minus):
    plus[:GROUPED] = a1[...]
    plus[GROUPED:] = b0[...]
    minus[:GROUPED] = b3[...]
    minus[GROUPED:] = a0[...]


def pieces_of(refs):
    if len(refs) == 4:
        a, b, c, d = refs
        return a, b, c, d
    plus, minus = refs
    low, high = pl.ds(0, GROUPED), pl.ds(GROUPED, GROUPED)
    return plus.at[low], minus.at[low], minus.at[high], plus.at[high]


def stack_weights_kernel(place, *refs):
    *pieces, own, other = refs
    y = place[2]
    for out, parts in ((own, pieces[:N]), (other, pieces[N:])):
        for k, w in enumerate(parts):
            block = wrap(y - k)
            for part in range(3):
                rows = pl.ds(pl.multiple_of(part * N * HID + block * HID, HID), HID)
                out[rows, :] = w[part * HID : (part + 1) * HID]


def split_columns_kernel(place, w, o0, o1, o2, o3):
    y = place[2]
    for k, o in enumerate((o0, o1, o2, o3)):
        o[...] = w[0, :, pl.ds(aligned(wrap(y + k) * EIGHTH), EIGHTH)]


def forward_kernel(place, *refs):
    *chunk, own, other, o0, o1, o2, o3, part = refs
    pieces = pieces_of(chunk)
    y, c = place[2], place[3]
    width = N * HID
    mine = pl.ds(aligned(c * EIGHTH), EIGHTH)
    theirs = pl.ds(aligned((1 - c) * EIGHTH), EIGHTH)
    for rows, span in (
        (slice(0, HELD), slice(0, 2 * width)),
        (slice(HELD, 2 * HELD), slice(2 * width, 3 * width)),
    ):
        v_mine = jnp.concatenate([v[rows, mine] for v in pieces], axis=0)
        v_theirs = jnp.concatenate([v[rows, theirs] for v in pieces], axis=0)
        part[:, span] = mm(v_mine, own[span], NT) + mm(v_theirs, other[span], NT)
    for k, o in enumerate((o0, o1, o2, o3)):
        at = wrap(y - k) * ROWS
        for s in range(2):
            rows = pl.ds(pl.multiple_of(s * GROUPED + at, ROWS), ROWS)
            o[s * ROWS : (s + 1) * ROWS] = part[rows, :].astype(o.dtype)


def middle_kernel(place, p0, p1, p2, p3, out):
    width = N * HID
    total = p0[...] + p1[...].astype(F32) + p2[...].astype(F32) + p3[...].astype(F32)
    pair = total[:, : 2 * width]
    d_hidden = total[:, 2 * width :]
    gate = pair[:, :width]
    up = pair[:, width:]
    sig = jax.nn.sigmoid(gate)
    act = gate * sig
    out[:, :width] = (d_hidden * up * sig * (1.0 + gate * (1.0 - sig))).astype(BF)
    out[:, width : 2 * width] = (d_hidden * act).astype(BF)
    out[:, 2 * width :] = (act * up).astype(BF)


def back_kernel(place, h0, h1, h2, h3, own, other, held, *outs):
    y, c = place[2], place[3]
    width = 2 * N * HID
    for k, h in enumerate((h0, h1, h2, h3)):
        at = wrap(y - k) * ROWS
        for s in range(2):
            rows = pl.ds(pl.multiple_of(s * GROUPED + at, ROWS), ROWS)
            held[rows, :] = h[s * ROWS : (s + 1) * ROWS]
    h = held[:, :width]
    for w, half in ((own, c), (other, 1 - c)):
        cols = pl.ds(aligned(half * EIGHTH), EIGHTH)
        part = mm(h, w[:width], NN)
        for i, o in enumerate(outs):
            o[:, cols] = part[i * HELD : (i + 1) * HELD].astype(BF)


def pass_on_kernel(place, own_a, own_b, got_a, got_b, out_a, out_b):
    out_a[...] = (own_a[...].astype(F32) + got_a[...].astype(F32)).astype(BF)
    out_b[...] = (own_b[...].astype(F32) + got_b[...].astype(F32)).astype(BF)


def weight_grad(half, h1, h2, chunks, out):
    pieces = (*pieces_of(chunks[:4]), *pieces_of(chunks[4:]))
    width = 2 * N * HID
    cols = pl.ds(aligned(half * EIGHTH), EIGHTH)
    hs = jnp.concatenate([h1[...], h2[...]], axis=0)
    x = jnp.concatenate([v[:HELD, cols] for v in pieces], axis=0)
    out[:width] = mm(hs[:, :width], x, TN).astype(out.dtype)
    g = jnp.concatenate([v[HELD : 2 * HELD, cols] for v in pieces], axis=0)
    out[width:] = mm(hs[:, width:], g, TN).astype(out.dtype)


def their_grad_kernel(place, h1, h2, *refs):
    *chunks, out = refs
    weight_grad(1 - place[3], h1, h2, chunks, out)


def my_grad_kernel(place, got, h1, h2, *refs):
    *chunks, o0, o1, o2, o3, mine = refs
    y = place[2]
    weight_grad(place[3], h1, h2, chunks, mine)
    for k, o in enumerate((o0, o1, o2, o3)):
        block = wrap(y - k)
        for part in range(3):
            rows = pl.ds(pl.multiple_of(part * N * HID + block * HID, HID), HID)
            total = mine[rows, :] + got[rows, :].astype(F32)
            o[part * HID : (part + 1) * HID] = total.astype(o.dtype)


def sum_back_kernel(place, own_a, own_b, got_a, got_b, out):
    for h, (own, got) in enumerate(((own_a, got_a), (own_b, got_b))):
        total = own[...].astype(F32) + got[...].astype(F32)
        for s in range(2):
            for x in range(N):
                at = s * ROWS + x * SLOT
                out[x * N + 2 * h + s] = total[at : at + SLOT].astype(BF)


def combine_kernel(place, pick, got, out):
    for q in range(N):
        rows = jnp.concatenate([got[e * N + q].astype(F32) for e in range(N)], axis=0)
        total = mm(pick[...], rows.astype(BF), TN).astype(BF)
        for c in range(2):
            at = c * HALF + q * EIGHTH
            out[:, at : at + EIGHTH] = total[:, c * EIGHTH : (c + 1) * EIGHTH]


def moments_kernel(place, g0, g1, g2, g3, one, two, new_one, new_two):
    step = pl.program_id(0)
    for k, g in enumerate((g0, g1, g2, g3)):

        @pl.when(step == k)
        def _():
            grad = g[...].astype(F32)
            new_one[0] = beta_one * one[0] + (1.0 - beta_one) * grad
            new_two[0] = beta_two * two[0] + (1.0 - beta_two) * grad * grad


def moments(place, grads, one, two):
    rows = one.shape[1]
    piece = pl.BlockSpec((rows, EIGHTH), lambda k, place: (0, 0))
    block = pl.BlockSpec((1, rows, EIGHTH), lambda k, place: (0, 0, lax.rem(place[2] + k, N)))
    return pl.pallas_call(
        moments_kernel,
        name="moments",
        grid_spec=pltpu.PrefetchScalarGridSpec(
            num_scalar_prefetch=1,
            grid=(N,),
            in_specs=[piece] * N + [block] * 2,
            out_specs=[block] * 2,
        ),
        out_shape=[jax.ShapeDtypeStruct(v.shape, v.dtype) for v in (one, two)],
        cost_estimate=pl.CostEstimate(
            flops=6 * one.size, bytes_accessed=17 * one.size, transcendentals=0
        ),
        compiler_params=pltpu.CompilerParams(vmem_limit_bytes=VMEM_MOST),
    )(place, *grads, one, two)


def exchange(value, axes):
    groups = {}
    for index in range(N * N * N):
        at = {"x": index // (N * N), "z": index // N % N, "y": index % N}
        groups.setdefault(tuple(at[a] for a in at if a not in axes), []).append(index)
    return lax.all_to_all(
        value, "expert", 0, 0, axis_index_groups=list(groups.values()), tiled=True
    )


def spread(parts, axis, sign=1):
    moved = {k: turn(parts[k], axis, sign * k) for k in (2, 1, 3)}
    return [parts[0]] + [moved[k] for k in range(1, N)]


def after(values, *earlier):
    return lax.optimization_barrier((values, earlier))[0]


def add(place, own_a, own_b, got_a, got_b):
    half = ((HELD, QUARTER), BF)
    return call(pass_on_kernel, "pass_on", [half] * 2, place, own_a, own_b, got_a, got_b)


def middle_part(place, chunk, w_own, w_other, *earlier):
    width = 3 * N * HID
    part = call(
        forward_kernel,
        "forward",
        [((HELD, width), F32)] + [((HELD, width), BF)] * 3,
        place,
        *chunk,
        w_own,
        w_other,
        flops=2 * CHUNK * QUARTER * width,
        scratch=[pltpu.VMEM((CHUNK, width), F32)],
    )
    part = after(spread(part, "y", -1), *earlier)
    (held,) = call(middle_kernel, "middle", [((HELD, width), BF)], place, *part)
    return held


def back_part(place, held, w_own, w_other):
    return call(
        back_kernel,
        "back",
        [((CHUNK, 3 * N * HID), BF)] + [((HELD, QUARTER), BF)] * 4,
        place,
        *held,
        w_own,
        w_other,
        flops=4 * CHUNK * QUARTER * N * HID,
    )


def shards(tokens, grad_out, gates, expert_ids, expert_weights, moment_one, moment_two):
    expert = lax.axis_index("expert")
    core = lax.axis_index("dp")
    place = jnp.stack([expert // (N * N), expert // N % N, expert % N, core]).astype(jnp.int32)
    tok = tokens.shape[0]
    width = N * HID
    slots = ((N * N, SLOT, QUARTER), BF)
    block_rows = expert_weights.shape[1]

    sent, pick = route(expert_ids.T, gates.T, tokens, grad_out)
    got = exchange(sent, "xy")
    w_columns = call(
        split_columns_kernel,
        "split_columns",
        [((block_rows, EIGHTH), BF)] * N,
        place,
        expert_weights,
    )
    w_parts = spread(after(w_columns, got), "y")
    got = after(got, w_columns[1])
    a0, b0 = call(pair_kernel, "pair", [((GROUPED, QUARTER), BF)] * 2, place, got)
    a1, b3 = turn(a0, "z", 1), turn(b0, "z", -1)
    first = a0, b0, a1, b3
    plus, minus = call(
        stack_kernel, "stack", [((2 * GROUPED, QUARTER), BF)] * 2, place, *first
    )
    w_parts = after(w_parts, plus)
    second = turn(plus, "z", 1), turn(minus, "z", -1)
    w_others = [turn(w, "c", 1) for w in w_parts]
    w_own, w_other = call(
        stack_weights_kernel,
        "stack_weights",
        [((N * block_rows, EIGHTH), BF)] * 2,
        place,
        *w_parts,
        *w_others,
    )

    mid_one = middle_part(place, first, w_own, w_other)
    held_one = spread([mid_one] * N, "y")
    held_one, r_a0, r_b0, r_a1, r_b3 = back_part(place, held_one, w_own, w_other)
    got_a, got_b = turn(r_a1, "z", 1), turn(r_b3, "z", -1)
    second = after(second, mid_one)
    held_two = middle_part(place, second, w_own, w_other, r_a1)
    held_two = after(spread([held_two] * N, "y"), got_a, got_b)
    held_two, r_a2, r_b2, r_a3, r_b1 = back_part(place, held_two, w_own, w_other)
    got_a, got_b = add(place, r_a2, r_b2, got_a, got_b)
    held = after((held_one, held_two), got_a)
    got_a, got_b = turn(got_a, "z", 1), turn(got_b, "z", -1)
    flops = N * GROUPED * QUARTER * 3 * width
    (grad_theirs,) = call(
        their_grad_kernel,
        "their_grad",
        [((3 * width, EIGHTH), BF)],
        place,
        *held,
        *first,
        *second,
        flops=flops,
    )
    grad_got = turn(grad_theirs, "c", 1)
    blocks = call(
        my_grad_kernel,
        "my_grad",
        [((block_rows, EIGHTH), F32)] + [((block_rows, EIGHTH), BF)] * 3,
        place,
        grad_got,
        *held,
        *first,
        *second,
        flops=flops,
        scratch=[pltpu.VMEM((3 * width, EIGHTH), F32)],
    )
    got_a, got_b = after((got_a, got_b), blocks[0])
    got_a, got_b = add(place, r_a3, r_b1, got_a, got_b)
    got_a, got_b = turn(got_a, "z", 1), turn(got_b, "z", -1)
    blocks = spread(blocks, "y", -1)
    got_a, got_b = after((got_a, got_b), *blocks)
    (back,) = call(sum_back_kernel, "sum_back", [slots], place, r_a0, r_b0, got_a, got_b)
    back = exchange(back, "xy")
    new_one, new_two = moments(place, blocks, moment_one, moment_two)
    back = after(back, new_one)
    (grad_tokens,) = call(
        combine_kernel,
        "combine",
        [((tok, D), BF)],
        place,
        pick,
        back,
        flops=2 * ROWS * tok * D,
    )
    return grad_tokens, new_one, new_two


def solution(mesh):
    return jax.shard_map(
        shards,
        mesh=mesh,
        in_specs=(
            P(("expert", "dp"), None),
            P(("expert", "dp"), None),
            P(("expert", "dp"), None),
            P(("expert", "dp"), None),
            P("expert", None, "dp"),
            P("expert", None, "dp"),
            P("expert", None, "dp"),
        ),
        out_specs=(P(("expert", "dp"), None), P("expert", None, "dp"), P("expert", None, "dp")),
        check_vma=False,
    )
```

```python
import functools

import jax
import jax.numpy as jnp
from jax import lax
from jax.experimental import pallas as pl
from jax.experimental.pallas import tpu as pltpu
from jax.sharding import PartitionSpec as P

N = 4
SLOT = 8
HID = 64
D = 7168
HALF = D // 2
EIGHTH = HALF // N
QUARTER = 2 * EIGHTH
ROWS = N * SLOT
GROUPED = N * ROWS
HELD = 2 * ROWS
CHUNK = N * HELD
BF = jnp.bfloat16
F32 = jnp.float32
VMEM_LIMIT = 16 * 1024 * 1024
VMEM_MOST = 56 * 1024 * 1024
beta_one = 0.9
beta_two = 0.95


def rotation(axis, step):
    pairs = []
    for x in range(N):
        for z in range(N):
            for y in range(N):
                for c in range(2):
                    to = {"x": x, "z": z, "y": y, "c": c}
                    to[axis] = (to[axis] + step) % (2 if axis == "c" else N)
                    source = ((x * N + z) * N + y) * 2 + c
                    target = ((to["x"] * N + to["z"]) * N + to["y"]) * 2 + to["c"]
                    pairs.append((source, target))
    return pairs


def turn(value, axis, step):
    return lax.ppermute(value, ("expert", "dp"), rotation(axis, step))


def call(kernel, name, outs, place, *ins, flops=0, scratch=(), own_copies=()):
    outs = [jax.ShapeDtypeStruct(s, t) for s, t in outs]
    size = sum(v.size * v.dtype.itemsize for v in (*ins, *outs))
    return pl.pallas_call(
        kernel,
        name=name,
        out_shape=outs,
        in_specs=[pl.BlockSpec(memory_space=pltpu.SMEM)]
        + [pl.BlockSpec(memory_space=pltpu.VMEM)] * len(ins),
        out_specs=[
            pl.BlockSpec(memory_space=pl.ANY if i in own_copies else pltpu.VMEM)
            for i in range(len(outs))
        ],
        scratch_shapes=list(scratch),
        cost_estimate=pl.CostEstimate(flops=flops, bytes_accessed=size, transcendentals=0),
        compiler_params=pltpu.CompilerParams(vmem_limit_bytes=VMEM_LIMIT),
    )(place, *ins)


def wrap(v):
    return lax.rem(v + 2 * N, N)


def aligned(v):
    return pl.multiple_of(v, 128)


def mm(a, b, dims):
    return lax.dot_general(a, b, (dims, ((), ())), preferred_element_type=F32)


NN = ((1,), (0,))
NT = ((1,), (1,))
TN = ((0,), (0,))


def route_kernel(
    ids_in, gates_in, tokens, grads, out, pick_out, ids, gates, tok_buf, grad_buf, sems
):
    tok = ids.shape[1]
    small = [
        pltpu.make_async_copy(ids_in, ids, sems.at[4 * N]),
        pltpu.make_async_copy(gates_in, gates, sems.at[4 * N + 1]),
    ]
    for copy in small:
        copy.start()
    copies = []
    for q in range(N):
        for i, (source, buf) in enumerate(((tokens, tok_buf), (grads, grad_buf))):
            for c in range(2):
                cols = pl.ds(c * HALF + q * EIGHTH, EIGHTH)
                copy = pltpu.make_async_copy(
                    source.at[:, cols], buf.at[:, cols], sems.at[q * 4 + i * 2 + c]
                )
                copy.start()
                copies.append(copy)
    row_i = lax.broadcasted_iota(jnp.int32, (tok, tok), 0)
    col_i = lax.broadcasted_iota(jnp.int32, (tok, tok), 1)
    slot = lax.broadcasted_iota(jnp.int32, (ROWS, tok), 0)
    for copy in small:
        copy.wait()
    idv = ids[...]
    gv = gates[...]
    hits = [idv == e for e in range(N)]
    members = [jnp.sum(h.astype(F32), axis=0, keepdims=True) for h in hits]
    chosen = [jnp.sum(jnp.where(h, gv, 0.0), axis=0, keepdims=True) for h in hits]
    mask = jnp.concatenate(members + [jnp.zeros((8 - N, tok), F32)], axis=0)
    before = mm(mask, (row_i < col_i).astype(F32), NN).astype(jnp.int32)
    place_of = jnp.zeros((ROWS, tok), jnp.int32)
    weight = jnp.zeros((ROWS, tok), F32)
    for e in range(N):
        spot = jnp.where(members[e] > 0.0, before[e : e + 1] + e * SLOT, -1)
        mine = slot // SLOT == e
        place_of = jnp.where(mine, spot, place_of)
        weight = jnp.where(mine, chosen[e], weight)
    on = place_of == slot
    pick = jnp.where(on, 1.0, 0.0).astype(BF)
    pick_out[...] = pick
    gate = jnp.sum(jnp.where(on, weight, 0.0), axis=1, keepdims=True)
    for q in range(N):
        for copy in copies[q * 4 : q * 4 + 4]:
            copy.wait()
        for c in range(2):
            cols = slice(c * HALF + q * EIGHTH, c * HALF + (q + 1) * EIGHTH)
            rows = mm(pick, tok_buf[:, cols], NN)
            scaled = mm(pick, grad_buf[:, cols], NN) * gate
            for e in range(N):
                at = slice(e * SLOT, (e + 1) * SLOT)
                both = jnp.concatenate([rows[at], scaled[at]], axis=0).astype(BF)
                out[e * N + q, :, c * EIGHTH : (c + 1) * EIGHTH] = both


def route(ids, gates, tokens, grad_out):
    tok = tokens.shape[0]
    vmem = pl.BlockSpec(memory_space=pltpu.VMEM)
    hbm = pl.BlockSpec(memory_space=pltpu.HBM)
    return pl.pallas_call(
        route_kernel,
        name="route",
        in_specs=[hbm] * 4,
        out_specs=[vmem, vmem],
        out_shape=[
            jax.ShapeDtypeStruct((N * N, 2 * SLOT, QUARTER), BF),
            jax.ShapeDtypeStruct((ROWS, tok), BF),
        ],
        scratch_shapes=[
            pltpu.VMEM(ids.shape, jnp.int32),
            pltpu.VMEM(gates.shape, F32),
            pltpu.VMEM((tok, D), BF),
            pltpu.VMEM((tok, D), BF),
            pltpu.SemaphoreType.DMA((4 * N + 2,)),
        ],
        cost_estimate=pl.CostEstimate(
            flops=4 * ROWS * tok * D, bytes_accessed=6 * tok * D, transcendentals=0
        ),
        compiler_params=pltpu.CompilerParams(vmem_limit_bytes=VMEM_MOST),
    )(ids, gates, tokens, grad_out)


def pair_kernel(place, got, a, b):
    for g in range(N):
        pieces = [got[x * N + g].astype(F32) for x in range(N)]
        for part in range(2):
            rows = [v[part * SLOT : (part + 1) * SLOT] for v in pieces]
            at = (part * 2 + g % 2) * ROWS
            (a, b)[g // 2][at : at + ROWS] = jnp.concatenate(rows, axis=0).astype(BF)


def stack_kernel(place, a0, b0, a1, b3, plus, minus):
    plus[:GROUPED] = a1[...]
    plus[GROUPED:] = b0[...]
    minus[:GROUPED] = b3[...]
    minus[GROUPED:] = a0[...]


def pieces_of(refs):
    if len(refs) == 4:
        a, b, c, d = refs
        return a, b, c, d
    plus, minus = refs
    low, high = pl.ds(0, GROUPED), pl.ds(GROUPED, GROUPED)
    return plus.at[low], minus.at[low], minus.at[high], plus.at[high]


def stack_weights_kernel(place, *refs):
    *pieces, own, other = refs
    y = place[2]
    for out, parts in ((own, pieces[:N]), (other, pieces[N:])):
        for k, w in enumerate(parts):
            block = wrap(y - k)
            for part in range(3):
                rows = pl.ds(pl.multiple_of(part * N * HID + block * HID, HID), HID)
                out[rows, :] = w[part * HID : (part + 1) * HID]


def split_columns_kernel(place, w, o0, o1, o2, o3):
    y = place[2]
    for k, o in enumerate((o0, o1, o2, o3)):
        o[...] = w[0, :, pl.ds(aligned(wrap(y + k) * EIGHTH), EIGHTH)]


def forward_kernel(place, *refs):
    *chunk, own, other, o0, o1, o2, o3, part = refs
    pieces = pieces_of(chunk)
    y, c = place[2], place[3]
    width = N * HID
    mine = pl.ds(aligned(c * EIGHTH), EIGHTH)
    theirs = pl.ds(aligned((1 - c) * EIGHTH), EIGHTH)
    for rows, span in (
        (slice(0, HELD), slice(0, 2 * width)),
        (slice(HELD, 2 * HELD), slice(2 * width, 3 * width)),
    ):
        v_mine = jnp.concatenate([v[rows, mine] for v in pieces], axis=0)
        v_theirs = jnp.concatenate([v[rows, theirs] for v in pieces], axis=0)
        part[:, span] = mm(v_mine, own[span], NT) + mm(v_theirs, other[span], NT)
    for k, o in enumerate((o0, o1, o2, o3)):
        at = wrap(y - k) * ROWS
        for s in range(2):
            rows = pl.ds(pl.multiple_of(s * GROUPED + at, ROWS), ROWS)
            o[s * ROWS : (s + 1) * ROWS] = part[rows, :].astype(o.dtype)


def middle_kernel(place, p0, p1, p2, p3, out):
    width = N * HID
    total = p0[...] + p1[...].astype(F32) + p2[...].astype(F32) + p3[...].astype(F32)
    pair = total[:, : 2 * width]
    d_hidden = total[:, 2 * width :]
    gate = pair[:, :width]
    up = pair[:, width:]
    sig = jax.nn.sigmoid(gate)
    act = gate * sig
    out[:, :width] = (d_hidden * up * sig * (1.0 + gate * (1.0 - sig))).astype(BF)
    out[:, width : 2 * width] = (d_hidden * act).astype(BF)
    out[:, 2 * width :] = (act * up).astype(BF)


def back_kernel(place, held, own, other, a0, b0, a1, b3, minus, plus):
    c = place[3]
    width = 2 * N * HID
    h = held[:, :width]
    low, high = slice(0, HELD), slice(HELD, 2 * HELD)
    targets = ((a0, low), (b0, low), (a1, low), (b3, low))
    targets += ((minus, low), (plus, low), (plus, high), (minus, high))
    for w, half in ((own, c), (other, 1 - c)):
        cols = pl.ds(aligned(half * EIGHTH), EIGHTH)
        part = mm(h, w[:width], NN)
        for i, (o, rows) in enumerate(targets):
            o[rows, cols] = part[i * HELD : (i + 1) * HELD].astype(BF)


def pass_on_kernel(place, own_a, own_b, got_a, got_b, out_a, out_b):
    out_a[...] = (own_a[...].astype(F32) + got_a[:HELD].astype(F32)).astype(BF)
    out_b[...] = (own_b[...].astype(F32) + got_b[:HELD].astype(F32)).astype(BF)


def weight_grad(half, held, chunks, out):
    pieces = (*pieces_of(chunks[:4]), *pieces_of(chunks[4:]))
    width = 2 * N * HID
    cols = pl.ds(aligned(half * EIGHTH), EIGHTH)
    x = jnp.concatenate([v[:HELD, cols] for v in pieces], axis=0)
    out[:width] = mm(held[:, :width], x, TN).astype(out.dtype)
    g = jnp.concatenate([v[HELD : 2 * HELD, cols] for v in pieces], axis=0)
    out[width:] = mm(held[:, width:], g, TN).astype(out.dtype)


def their_grad_kernel(place, *refs):
    parts = refs[:N], refs[N : 2 * N]
    *chunks, held, o0, o1, o2, theirs = refs[2 * N :]
    y = place[2]
    for i, chunk in enumerate(parts):
        for k, h in enumerate(chunk):
            at = wrap(y - k) * ROWS
            for s in range(2):
                rows = pl.ds(pl.multiple_of(i * CHUNK + s * GROUPED + at, ROWS), ROWS)
                held[rows, :] = h[s * ROWS : (s + 1) * ROWS]
    weight_grad(1 - place[3], held, chunks, theirs)
    for i, o in enumerate((o0, o1, o2)):
        o[...] = theirs[i * N * HID : (i + 1) * N * HID]


def my_grad_kernel(place, got0, got1, got2, held, *refs):
    *chunks, o0, o1, o2, o3, mine = refs
    y = place[2]
    weight_grad(place[3], held, chunks, mine)
    for k, o in enumerate((o0, o1, o2, o3)):
        block = pl.multiple_of(wrap(y - k) * HID, HID)
        for part, got in enumerate((got0, got1, got2)):
            own = mine[pl.ds(pl.multiple_of(part * N * HID + block, HID), HID), :]
            total = own + got[pl.ds(block, HID), :].astype(F32)
            o[part * HID : (part + 1) * HID] = total.astype(o.dtype)


def sum_back_kernel(place, a0, b0, a1, b3, got_minus, got_plus, out):
    for h, (i, j, k) in enumerate(((a0, a1, got_plus), (b0, b3, got_minus))):
        total = i[...].astype(F32) + (j[...].astype(F32) + k[HELD:].astype(F32))
        for s in range(2):
            for x in range(N):
                at = s * ROWS + x * SLOT
                out[x * N + 2 * h + s] = total[at : at + SLOT].astype(BF)


def combine_kernel(place, pick, got, out, sums, sems):
    copies = []
    for q in range(N):
        rows = jnp.concatenate([got[e * N + q].astype(F32) for e in range(N)], axis=0)
        sums[q] = mm(pick[...], rows.astype(BF), TN).astype(BF)
        for c in range(2):
            copy = pltpu.make_async_copy(
                sums.at[q, :, pl.ds(c * EIGHTH, EIGHTH)],
                out.at[:, pl.ds(c * HALF + q * EIGHTH, EIGHTH)],
                sems.at[q * 2 + c],
            )
            copy.start()
            copies.append(copy)
    for copy in copies:
        copy.wait()


def moments_kernel(place, g0, g1, g2, g3, one, two, new_one, new_two):
    step = pl.program_id(0)
    for k, g in enumerate((g0, g1, g2, g3)):

        @pl.when(step == k)
        def _():
            grad = g[...].astype(F32)
            new_one[0] = beta_one * one[0] + (1.0 - beta_one) * grad
            new_two[0] = beta_two * two[0] + (1.0 - beta_two) * grad * grad


def moments(place, grads, one, two):
    rows = one.shape[1]
    piece = pl.BlockSpec((rows, EIGHTH), lambda k, place: (0, 0))
    block = pl.BlockSpec((1, rows, EIGHTH), lambda k, place: (0, 0, lax.rem(place[2] + k, N)))
    return pl.pallas_call(
        moments_kernel,
        name="moments",
        grid_spec=pltpu.PrefetchScalarGridSpec(
            num_scalar_prefetch=1,
            grid=(N,),
            in_specs=[piece] * N + [block] * 2,
            out_specs=[block] * 2,
        ),
        out_shape=[jax.ShapeDtypeStruct(v.shape, v.dtype) for v in (one, two)],
        cost_estimate=pl.CostEstimate(
            flops=6 * one.size, bytes_accessed=17 * one.size, transcendentals=0
        ),
        compiler_params=pltpu.CompilerParams(vmem_limit_bytes=VMEM_MOST),
    )(place, *grads, one, two)


def exchange(value, axes):
    groups = {}
    for index in range(N * N * N):
        at = {"x": index // (N * N), "z": index // N % N, "y": index % N}
        groups.setdefault(tuple(at[a] for a in at if a not in axes), []).append(index)
    return lax.all_to_all(
        value, "expert", 0, 0, axis_index_groups=list(groups.values()), tiled=True
    )


def spread(parts, axis, sign=1):
    moved = {k: turn(parts[k], axis, sign * k) for k in (2, 1, 3)}
    return [parts[0]] + [moved[k] for k in range(1, N)]


def after(values, *earlier):
    return lax.optimization_barrier((values, earlier))[0]


def pass_on(place, *parts):
    half = ((HELD, QUARTER), BF)
    return call(pass_on_kernel, "pass_on", [half] * 2, place, *parts)


def forward_part(place, chunk, w_own, w_other):
    width = 3 * N * HID
    return call(
        forward_kernel,
        "forward",
        [((HELD, width), F32)] + [((HELD, width), BF)] * 3,
        place,
        *chunk,
        w_own,
        w_other,
        flops=2 * CHUNK * QUARTER * width,
        scratch=[pltpu.VMEM((CHUNK, width), F32)],
    )


def middle_part(place, part):
    return call(middle_kernel, "middle", [((HELD, 3 * N * HID), BF)], place, *part)[0]


def back_part(place, held, w_own, w_other):
    return call(
        back_kernel,
        "back",
        [((HELD, QUARTER), BF)] * 4 + [((2 * HELD, QUARTER), BF)] * 2,
        place,
        held,
        w_own,
        w_other,
        flops=8 * CHUNK * QUARTER * N * HID,
    )


def shards(tokens, grad_out, gates, expert_ids, expert_weights, moment_one, moment_two):
    expert = lax.axis_index("expert")
    core = lax.axis_index("dp")
    place = jnp.stack([expert // (N * N), expert // N % N, expert % N, core]).astype(jnp.int32)
    tok = tokens.shape[0]
    width = N * HID
    slots = ((N * N, SLOT, QUARTER), BF)
    block_rows = expert_weights.shape[1]

    sent, pick = route(expert_ids.T, gates.T, tokens, grad_out)
    got = exchange(sent, "xy")
    w_columns = call(
        split_columns_kernel,
        "split_columns",
        [((block_rows, EIGHTH), BF)] * N,
        place,
        expert_weights,
    )
    w_parts = spread(w_columns, "y")
    got = after(got, w_columns[1])
    a0, b0 = call(pair_kernel, "pair", [((GROUPED, QUARTER), BF)] * 2, place, got)
    a1, b3 = turn(a0, "z", 1), turn(b0, "z", -1)
    first = a0, b0, a1, b3
    plus, minus = call(
        stack_kernel, "stack", [((2 * GROUPED, QUARTER), BF)] * 2, place, *first
    )
    w_parts = after(w_parts, plus)
    second = turn(plus, "z", 1), turn(minus, "z", -1)
    w_others = [turn(w, "c", 1) for w in w_parts]
    w_own, w_other = call(
        stack_weights_kernel,
        "stack_weights",
        [((N * block_rows, EIGHTH), BF)] * 2,
        place,
        *w_parts,
        *w_others,
    )

    part_one = forward_part(place, first, w_own, w_other)
    part_one = spread(part_one, "y", -1)
    part_two = forward_part(place, second, w_own, w_other)
    part_one = after(part_one, part_two[1])
    part_two = spread(part_two, "y", -1)
    mid_one = middle_part(place, part_one)
    held_one = spread([mid_one] * N, "y")
    mid_two = middle_part(place, part_two)
    held_two = spread([mid_two] * N, "y")
    flops = N * GROUPED * QUARTER * 3 * width
    held, *theirs = call(
        their_grad_kernel,
        "their_grad",
        [((2 * CHUNK, 3 * width), BF)] + [((width, EIGHTH), BF)] * 3,
        place,
        *held_one,
        *held_two,
        *first,
        *second,
        flops=flops,
        scratch=[pltpu.VMEM((3 * width, EIGHTH), BF)],
    )
    a0, b0, a1, b3, minus, plus = back_part(place, held, w_own, w_other)
    got_minus, got_plus = turn(minus, "z", -1), turn(plus, "z", 1)
    got = [turn(v, "c", 1) for v in theirs]
    blocks = call(
        my_grad_kernel,
        "my_grad",
        [((block_rows, EIGHTH), F32)] + [((block_rows, EIGHTH), BF)] * 3,
        place,
        *got,
        after(held, a1),
        *first,
        *second,
        flops=flops,
        scratch=[pltpu.VMEM((3 * width, EIGHTH), F32)],
    )
    a1, b3 = pass_on(place, *after((a1, b3, got_minus, got_plus), blocks[0]))
    a1, b3 = turn(a1, "z", -1), turn(b3, "z", 1)
    blocks = spread(blocks, "y", -1)
    parts = after((a0, b0, a1, b3, got_minus, got_plus), *blocks)
    (back,) = call(sum_back_kernel, "sum_back", [slots], place, *parts)
    back = exchange(back, "xy")
    new_one, new_two = moments(place, blocks, moment_one, moment_two)
    back = after(back, new_one)
    (grad_tokens,) = call(
        combine_kernel,
        "combine",
        [((tok, D), BF)],
        place,
        pick,
        back,
        flops=2 * ROWS * tok * D,
        scratch=[pltpu.VMEM((N, tok, QUARTER), BF), pltpu.SemaphoreType.DMA((2 * N,))],
        own_copies=(0,),
    )
    return grad_tokens, new_one, new_two


def solution(mesh):
    return jax.shard_map(
        shards,
        mesh=mesh,
        in_specs=(
            P(("expert", "dp"), None),
            P(("expert", "dp"), None),
            P(("expert", "dp"), None),
            P(("expert", "dp"), None),
            P("expert", None, "dp"),
            P("expert", None, "dp"),
            P("expert", None, "dp"),
        ),
        out_specs=(P(("expert", "dp"), None), P("expert", None, "dp"), P("expert", None, "dp")),
        check_vma=False,
    )
```

```python
import functools

import jax
import jax.numpy as jnp
from jax import lax
from jax.experimental import pallas as pl
from jax.experimental.pallas import tpu as pltpu
from jax.sharding import PartitionSpec as P

N = 4
SLOT = 8
HID = 64
D = 7168
HALF = D // 2
EIGHTH = HALF // N
QUARTER = 2 * EIGHTH
ROWS = N * SLOT
GROUPED = N * ROWS
HELD = 2 * ROWS
CHUNK = N * HELD
BF = jnp.bfloat16
F32 = jnp.float32
VMEM_LIMIT = 16 * 1024 * 1024
VMEM_MOST = 56 * 1024 * 1024
beta_one = 0.9
beta_two = 0.95


def rotation(axis, step):
    pairs = []
    for x in range(N):
        for z in range(N):
            for y in range(N):
                for c in range(2):
                    to = {"x": x, "z": z, "y": y, "c": c}
                    to[axis] = (to[axis] + step) % (2 if axis == "c" else N)
                    source = ((x * N + z) * N + y) * 2 + c
                    target = ((to["x"] * N + to["z"]) * N + to["y"]) * 2 + to["c"]
                    pairs.append((source, target))
    return pairs


def turn(value, axis, step):
    return lax.ppermute(value, ("expert", "dp"), rotation(axis, step))


def call(kernel, name, outs, place, *ins, flops=0, scratch=(), own_copies=()):
    outs = [jax.ShapeDtypeStruct(s, t) for s, t in outs]
    size = sum(v.size * v.dtype.itemsize for v in (*ins, *outs))
    return pl.pallas_call(
        kernel,
        name=name,
        out_shape=outs,
        in_specs=[pl.BlockSpec(memory_space=pltpu.SMEM)]
        + [pl.BlockSpec(memory_space=pltpu.VMEM)] * len(ins),
        out_specs=[
            pl.BlockSpec(memory_space=pl.ANY if i in own_copies else pltpu.VMEM)
            for i in range(len(outs))
        ],
        scratch_shapes=list(scratch),
        cost_estimate=pl.CostEstimate(flops=flops, bytes_accessed=size, transcendentals=0),
        compiler_params=pltpu.CompilerParams(vmem_limit_bytes=VMEM_LIMIT),
    )(place, *ins)


def wrap(v):
    return lax.rem(v + 2 * N, N)


def aligned(v):
    return pl.multiple_of(v, 128)


def mm(a, b, dims):
    return lax.dot_general(a, b, (dims, ((), ())), preferred_element_type=F32)


NN = ((1,), (0,))
NT = ((1,), (1,))
TN = ((0,), (0,))


def route_kernel(
    ids_in, gates_in, tokens, grads, out, pick_out, ids, gates, tok_buf, grad_buf, sems
):
    tok = ids.shape[1]
    small = [
        pltpu.make_async_copy(ids_in, ids, sems.at[4 * N]),
        pltpu.make_async_copy(gates_in, gates, sems.at[4 * N + 1]),
    ]
    for copy in small:
        copy.start()
    copies = []
    for q in range(N):
        for i, (source, buf) in enumerate(((tokens, tok_buf), (grads, grad_buf))):
            for c in range(2):
                cols = pl.ds(c * HALF + q * EIGHTH, EIGHTH)
                copy = pltpu.make_async_copy(
                    source.at[:, cols], buf.at[:, cols], sems.at[q * 4 + i * 2 + c]
                )
                copy.start()
                copies.append(copy)
    row_i = lax.broadcasted_iota(jnp.int32, (tok, tok), 0)
    col_i = lax.broadcasted_iota(jnp.int32, (tok, tok), 1)
    slot = lax.broadcasted_iota(jnp.int32, (ROWS, tok), 0)
    for copy in small:
        copy.wait()
    idv = ids[...]
    gv = gates[...]
    hits = [idv == e for e in range(N)]
    members = [jnp.sum(h.astype(F32), axis=0, keepdims=True) for h in hits]
    chosen = [jnp.sum(jnp.where(h, gv, 0.0), axis=0, keepdims=True) for h in hits]
    mask = jnp.concatenate(members + [jnp.zeros((8 - N, tok), F32)], axis=0)
    before = mm(mask, (row_i < col_i).astype(F32), NN).astype(jnp.int32)
    place_of = jnp.zeros((ROWS, tok), jnp.int32)
    weight = jnp.zeros((ROWS, tok), F32)
    for e in range(N):
        spot = jnp.where(members[e] > 0.0, before[e : e + 1] + e * SLOT, -1)
        mine = slot // SLOT == e
        place_of = jnp.where(mine, spot, place_of)
        weight = jnp.where(mine, chosen[e], weight)
    on = place_of == slot
    pick = jnp.where(on, 1.0, 0.0).astype(BF)
    pick_out[...] = pick
    gate = jnp.sum(jnp.where(on, weight, 0.0), axis=1, keepdims=True)
    for q in range(N):
        for copy in copies[q * 4 : q * 4 + 4]:
            copy.wait()
        for c in range(2):
            cols = slice(c * HALF + q * EIGHTH, c * HALF + (q + 1) * EIGHTH)
            rows = mm(pick, tok_buf[:, cols], NN)
            scaled = mm(pick, grad_buf[:, cols], NN) * gate
            for e in range(N):
                at = slice(e * SLOT, (e + 1) * SLOT)
                both = jnp.concatenate([rows[at], scaled[at]], axis=0).astype(BF)
                out[e * N + q, :, c * EIGHTH : (c + 1) * EIGHTH] = both


def route(ids, gates, tokens, grad_out):
    tok = tokens.shape[0]
    vmem = pl.BlockSpec(memory_space=pltpu.VMEM)
    hbm = pl.BlockSpec(memory_space=pltpu.HBM)
    return pl.pallas_call(
        route_kernel,
        name="route",
        in_specs=[hbm] * 4,
        out_specs=[vmem, vmem],
        out_shape=[
            jax.ShapeDtypeStruct((N * N, 2 * SLOT, QUARTER), BF),
            jax.ShapeDtypeStruct((ROWS, tok), BF),
        ],
        scratch_shapes=[
            pltpu.VMEM(ids.shape, jnp.int32),
            pltpu.VMEM(gates.shape, F32),
            pltpu.VMEM((tok, D), BF),
            pltpu.VMEM((tok, D), BF),
            pltpu.SemaphoreType.DMA((4 * N + 2,)),
        ],
        cost_estimate=pl.CostEstimate(
            flops=4 * ROWS * tok * D, bytes_accessed=6 * tok * D, transcendentals=0
        ),
        compiler_params=pltpu.CompilerParams(vmem_limit_bytes=VMEM_MOST),
    )(ids, gates, tokens, grad_out)


def pair_kernel(place, got, a, b):
    for g in range(N):
        pieces = [got[x * N + g].astype(F32) for x in range(N)]
        for part in range(2):
            rows = [v[part * SLOT : (part + 1) * SLOT] for v in pieces]
            at = (part * 2 + g % 2) * ROWS
            (a, b)[g // 2][at : at + ROWS] = jnp.concatenate(rows, axis=0).astype(BF)


def stack_kernel(place, a0, b0, a1, b3, plus, minus):
    plus[:GROUPED] = a1[...]
    plus[GROUPED:] = b0[...]
    minus[:GROUPED] = b3[...]
    minus[GROUPED:] = a0[...]


def pieces_of(refs):
    if len(refs) == 4:
        a, b, c, d = refs
        return a, b, c, d
    plus, minus = refs
    low, high = pl.ds(0, GROUPED), pl.ds(GROUPED, GROUPED)
    return plus.at[low], minus.at[low], minus.at[high], plus.at[high]


def stack_weights_kernel(place, *refs):
    *pieces, own, other = refs
    y = place[2]
    for out, parts in ((own, pieces[:N]), (other, pieces[N:])):
        for k, w in enumerate(parts):
            block = wrap(y - k)
            for part in range(3):
                rows = pl.ds(pl.multiple_of(part * N * HID + block * HID, HID), HID)
                out[rows, :] = w[part * HID : (part + 1) * HID]


def split_columns_kernel(place, w, o0, o1, o2, o3):
    y = place[2]
    for k, o in enumerate((o0, o1, o2, o3)):
        o[...] = w[0, :, pl.ds(aligned(wrap(y + k) * EIGHTH), EIGHTH)]


def forward_kernel(place, *refs):
    *chunk, own, other, o0, o1, o2, o3, part = refs
    pieces = pieces_of(chunk)
    y, c = place[2], place[3]
    width = N * HID
    mine = pl.ds(aligned(c * EIGHTH), EIGHTH)
    theirs = pl.ds(aligned((1 - c) * EIGHTH), EIGHTH)
    for rows, span in (
        (slice(0, HELD), slice(0, 2 * width)),
        (slice(HELD, 2 * HELD), slice(2 * width, 3 * width)),
    ):
        v_mine = jnp.concatenate([v[rows, mine] for v in pieces], axis=0)
        v_theirs = jnp.concatenate([v[rows, theirs] for v in pieces], axis=0)
        part[:, span] = mm(v_mine, own[span], NT) + mm(v_theirs, other[span], NT)
    for k, o in enumerate((o0, o1, o2, o3)):
        at = wrap(y - k) * ROWS
        for s in range(2):
            rows = pl.ds(pl.multiple_of(s * GROUPED + at, ROWS), ROWS)
            o[s * ROWS : (s + 1) * ROWS] = part[rows, :].astype(o.dtype)


def middle_kernel(place, p0, p1, p2, p3, out):
    width = N * HID
    total = p0[...] + p1[...].astype(F32) + p2[...].astype(F32) + p3[...].astype(F32)
    pair = total[:, : 2 * width]
    d_hidden = total[:, 2 * width :]
    gate = pair[:, :width]
    up = pair[:, width:]
    sig = jax.nn.sigmoid(gate)
    act = gate * sig
    out[:, :width] = (d_hidden * up * sig * (1.0 + gate * (1.0 - sig))).astype(BF)
    out[:, width : 2 * width] = (d_hidden * act).astype(BF)
    out[:, 2 * width :] = (act * up).astype(BF)


def back_kernel(first, place, held, own, other, *outs):
    c = place[3]
    width = 2 * N * HID
    h = held[first : first + CHUNK, :width]
    if len(outs) == 2:
        minus, plus = outs
        targets = (minus, 0), (plus, 0), (plus, HELD), (minus, HELD)
    else:
        targets = [(o, 0) for o in outs]
    for w, half in ((own, c), (other, 1 - c)):
        cols = pl.ds(aligned(half * EIGHTH), EIGHTH)
        part = mm(h, w[:width], NN)
        for i, (o, at) in enumerate(targets):
            o[at : at + HELD, cols] = part[i * HELD : (i + 1) * HELD].astype(BF)


def pass_on_kernel(place, own_a, own_b, got_a, got_b, out_a, out_b):
    out_a[...] = (own_a[...].astype(F32) + got_a[:HELD].astype(F32)).astype(BF)
    out_b[...] = (own_b[...].astype(F32) + got_b[:HELD].astype(F32)).astype(BF)


def weight_grad(half, held, chunks, out):
    pieces = (*pieces_of(chunks[:4]), *pieces_of(chunks[4:]))
    width = 2 * N * HID
    cols = pl.ds(aligned(half * EIGHTH), EIGHTH)
    x = jnp.concatenate([v[:HELD, cols] for v in pieces], axis=0)
    out[:width] = mm(held[:, :width], x, TN).astype(out.dtype)
    g = jnp.concatenate([v[HELD : 2 * HELD, cols] for v in pieces], axis=0)
    out[width:] = mm(held[:, width:], g, TN).astype(out.dtype)


def their_grad_kernel(place, *refs):
    parts = refs[:N], refs[N : 2 * N]
    *chunks, held, o0, o1, o2, theirs = refs[2 * N :]
    y = place[2]
    for i, chunk in enumerate(parts):
        for k, h in enumerate(chunk):
            at = wrap(y - k) * ROWS
            for s in range(2):
                rows = pl.ds(pl.multiple_of(i * CHUNK + s * GROUPED + at, ROWS), ROWS)
                held[rows, :] = h[s * ROWS : (s + 1) * ROWS]
    weight_grad(1 - place[3], held, chunks, theirs)
    for i, o in enumerate((o0, o1, o2)):
        o[...] = theirs[i * N * HID : (i + 1) * N * HID]


def my_grad_kernel(place, got0, got1, got2, held, *refs):
    *chunks, o0, o1, o2, o3, mine = refs
    y = place[2]
    weight_grad(place[3], held, chunks, mine)
    for k, o in enumerate((o0, o1, o2, o3)):
        block = pl.multiple_of(wrap(y - k) * HID, HID)
        for part, got in enumerate((got0, got1, got2)):
            own = mine[pl.ds(pl.multiple_of(part * N * HID + block, HID), HID), :]
            total = own + got[pl.ds(block, HID), :].astype(F32)
            o[part * HID : (part + 1) * HID] = total.astype(o.dtype)


def sum_back_kernel(place, a0, b0, a1, b3, got_minus, got_plus, out):
    for h, (i, j, k) in enumerate(((a0, a1, got_plus), (b0, b3, got_minus))):
        total = i[...].astype(F32) + (j[...].astype(F32) + k[HELD:].astype(F32))
        for s in range(2):
            for x in range(N):
                at = s * ROWS + x * SLOT
                out[x * N + 2 * h + s] = total[at : at + SLOT].astype(BF)


def combine_kernel(place, pick, got, out, sums, sems):
    copies = []
    for q in range(N):
        rows = jnp.concatenate([got[e * N + q].astype(F32) for e in range(N)], axis=0)
        sums[q] = mm(pick[...], rows.astype(BF), TN).astype(BF)
        for c in range(2):
            copy = pltpu.make_async_copy(
                sums.at[q, :, pl.ds(c * EIGHTH, EIGHTH)],
                out.at[:, pl.ds(c * HALF + q * EIGHTH, EIGHTH)],
                sems.at[q * 2 + c],
            )
            copy.start()
            copies.append(copy)
    for copy in copies:
        copy.wait()


def moments_kernel(place, g0, g1, g2, g3, one, two, new_one, new_two):
    step = pl.program_id(0)
    for k, g in enumerate((g0, g1, g2, g3)):

        @pl.when(step == k)
        def _():
            grad = g[...].astype(F32)
            new_one[0] = beta_one * one[0] + (1.0 - beta_one) * grad
            new_two[0] = beta_two * two[0] + (1.0 - beta_two) * grad * grad


def moments(place, grads, one, two):
    rows = one.shape[1]
    piece = pl.BlockSpec((rows, EIGHTH), lambda k, place: (0, 0))
    block = pl.BlockSpec((1, rows, EIGHTH), lambda k, place: (0, 0, lax.rem(place[2] + k, N)))
    return pl.pallas_call(
        moments_kernel,
        name="moments",
        grid_spec=pltpu.PrefetchScalarGridSpec(
            num_scalar_prefetch=1,
            grid=(N,),
            in_specs=[piece] * N + [block] * 2,
            out_specs=[block] * 2,
        ),
        out_shape=[jax.ShapeDtypeStruct(v.shape, v.dtype) for v in (one, two)],
        cost_estimate=pl.CostEstimate(
            flops=6 * one.size, bytes_accessed=17 * one.size, transcendentals=0
        ),
        compiler_params=pltpu.CompilerParams(vmem_limit_bytes=VMEM_MOST),
    )(place, *grads, one, two)


def exchange(value, axes):
    groups = {}
    for index in range(N * N * N):
        at = {"x": index // (N * N), "z": index // N % N, "y": index % N}
        groups.setdefault(tuple(at[a] for a in at if a not in axes), []).append(index)
    return lax.all_to_all(
        value, "expert", 0, 0, axis_index_groups=list(groups.values()), tiled=True
    )


def spread(parts, axis, sign=1):
    moved = {k: turn(parts[k], axis, sign * k) for k in (2, 1, 3)}
    return [parts[0]] + [moved[k] for k in range(1, N)]


def after(values, *earlier):
    return lax.optimization_barrier((values, earlier))[0]


def pass_on(place, *parts):
    half = ((HELD, QUARTER), BF)
    return call(pass_on_kernel, "pass_on", [half] * 2, place, *parts)


def forward_part(place, chunk, w_own, w_other):
    width = 3 * N * HID
    return call(
        forward_kernel,
        "forward",
        [((HELD, width), F32)] + [((HELD, width), BF)] * 3,
        place,
        *chunk,
        w_own,
        w_other,
        flops=2 * CHUNK * QUARTER * width,
        scratch=[pltpu.VMEM((CHUNK, width), F32)],
    )


def middle_part(place, part):
    return call(middle_kernel, "middle", [((HELD, 3 * N * HID), BF)], place, *part)[0]


def back_part(place, held, w_own, w_other, chunk):
    shape = (HELD, QUARTER) if chunk == 0 else (2 * HELD, QUARTER)
    return call(
        functools.partial(back_kernel, chunk * CHUNK),
        "back",
        [(shape, BF)] * (CHUNK // shape[0]),
        place,
        held,
        w_own,
        w_other,
        flops=4 * CHUNK * QUARTER * N * HID,
    )


def shards(tokens, grad_out, gates, expert_ids, expert_weights, moment_one, moment_two):
    expert = lax.axis_index("expert")
    core = lax.axis_index("dp")
    place = jnp.stack([expert // (N * N), expert // N % N, expert % N, core]).astype(jnp.int32)
    tok = tokens.shape[0]
    width = N * HID
    slots = ((N * N, SLOT, QUARTER), BF)
    block_rows = expert_weights.shape[1]

    sent, pick = route(expert_ids.T, gates.T, tokens, grad_out)
    got = exchange(sent, "xy")
    w_columns = call(
        split_columns_kernel,
        "split_columns",
        [((block_rows, EIGHTH), BF)] * N,
        place,
        expert_weights,
    )
    w_parts = spread(w_columns, "y")
    got = after(got, w_columns[1])
    a0, b0 = call(pair_kernel, "pair", [((GROUPED, QUARTER), BF)] * 2, place, got)
    a1, b3 = turn(a0, "z", 1), turn(b0, "z", -1)
    first = a0, b0, a1, b3
    plus, minus = call(
        stack_kernel, "stack", [((2 * GROUPED, QUARTER), BF)] * 2, place, *first
    )
    w_parts = after(w_parts, plus)
    second = turn(plus, "z", 1), turn(minus, "z", -1)
    w_others = [turn(w, "c", 1) for w in w_parts]
    w_own, w_other = call(
        stack_weights_kernel,
        "stack_weights",
        [((N * block_rows, EIGHTH), BF)] * 2,
        place,
        *w_parts,
        *w_others,
    )

    part_one = forward_part(place, first, w_own, w_other)
    part_one = spread(part_one, "y", -1)
    part_two = forward_part(place, second, w_own, w_other)
    part_one = after(part_one, part_two[1])
    part_two = spread(part_two, "y", -1)
    mid_one = middle_part(place, part_one)
    held_one = spread([mid_one] * N, "y")
    mid_two = middle_part(place, part_two)
    held_two = spread([mid_two] * N, "y")
    flops = N * GROUPED * QUARTER * 3 * width
    held, *theirs = call(
        their_grad_kernel,
        "their_grad",
        [((2 * CHUNK, 3 * width), BF)] + [((width, EIGHTH), BF)] * 3,
        place,
        *held_one,
        *held_two,
        *first,
        *second,
        flops=flops,
        scratch=[pltpu.VMEM((3 * width, EIGHTH), BF)],
    )
    minus, plus = back_part(place, held, w_own, w_other, 1)
    got_minus, got_plus = turn(minus, "z", -1), turn(plus, "z", 1)
    got = [turn(v, "c", 1) for v in theirs]
    blocks = call(
        my_grad_kernel,
        "my_grad",
        [((block_rows, EIGHTH), F32)] + [((block_rows, EIGHTH), BF)] * 3,
        place,
        *got,
        after(held, minus),
        *first,
        *second,
        flops=flops,
        scratch=[pltpu.VMEM((3 * width, EIGHTH), F32)],
    )
    a0, b0, a1, b3 = back_part(place, after(held, blocks[0]), w_own, w_other, 0)
    a1, b3 = pass_on(place, *after((a1, b3, got_minus, got_plus), blocks[0]))
    a1, b3 = turn(a1, "z", -1), turn(b3, "z", 1)
    blocks = spread(blocks, "y", -1)
    parts = after((a0, b0, a1, b3, got_minus, got_plus), *blocks)
    (back,) = call(sum_back_kernel, "sum_back", [slots], place, *parts)
    back = exchange(back, "xy")
    new_one, new_two = moments(place, blocks, moment_one, moment_two)
    back = after(back, new_one)
    (grad_tokens,) = call(
        combine_kernel,
        "combine",
        [((tok, D), BF)],
        place,
        pick,
        back,
        flops=2 * ROWS * tok * D,
        scratch=[pltpu.VMEM((N, tok, QUARTER), BF), pltpu.SemaphoreType.DMA((2 * N,))],
        own_copies=(0,),
    )
    return grad_tokens, new_one, new_two


def solution(mesh):
    return jax.shard_map(
        shards,
        mesh=mesh,
        in_specs=(
            P(("expert", "dp"), None),
            P(("expert", "dp"), None),
            P(("expert", "dp"), None),
            P(("expert", "dp"), None),
            P("expert", None, "dp"),
            P("expert", None, "dp"),
            P("expert", None, "dp"),
        ),
        out_specs=(P(("expert", "dp"), None), P("expert", None, "dp"), P("expert", None, "dp")),
        check_vma=False,
    )
```

```python
import functools

import jax
import jax.numpy as jnp
from jax import lax
from jax.experimental import pallas as pl
from jax.experimental.pallas import tpu as pltpu
from jax.sharding import PartitionSpec as P

N = 4
SLOT = 8
HID = 64
D = 7168
HALF = D // 2
EIGHTH = HALF // N
QUARTER = 2 * EIGHTH
ROWS = N * SLOT
GROUPED = N * ROWS
HELD = 2 * ROWS
CHUNK = N * HELD
BF = jnp.bfloat16
F32 = jnp.float32
VMEM_LIMIT = 16 * 1024 * 1024
VMEM_MOST = 56 * 1024 * 1024
beta_one = 0.9
beta_two = 0.95


def rotation(axis, step):
    pairs = []
    for x in range(N):
        for z in range(N):
            for y in range(N):
                for c in range(2):
                    to = {"x": x, "z": z, "y": y, "c": c}
                    to[axis] = (to[axis] + step) % (2 if axis == "c" else N)
                    source = ((x * N + z) * N + y) * 2 + c
                    target = ((to["x"] * N + to["z"]) * N + to["y"]) * 2 + to["c"]
                    pairs.append((source, target))
    return pairs


def turn(value, axis, step):
    return lax.ppermute(value, ("expert", "dp"), rotation(axis, step))


def call(kernel, name, outs, place, *ins, flops=0, scratch=(), own_copies=()):
    outs = [jax.ShapeDtypeStruct(s, t) for s, t in outs]
    size = sum(v.size * v.dtype.itemsize for v in (*ins, *outs))
    return pl.pallas_call(
        kernel,
        name=name,
        out_shape=outs,
        in_specs=[pl.BlockSpec(memory_space=pltpu.SMEM)]
        + [pl.BlockSpec(memory_space=pltpu.VMEM)] * len(ins),
        out_specs=[
            pl.BlockSpec(memory_space=pl.ANY if i in own_copies else pltpu.VMEM)
            for i in range(len(outs))
        ],
        scratch_shapes=list(scratch),
        cost_estimate=pl.CostEstimate(flops=flops, bytes_accessed=size, transcendentals=0),
        compiler_params=pltpu.CompilerParams(vmem_limit_bytes=VMEM_LIMIT),
    )(place, *ins)


def wrap(v):
    return lax.rem(v + 2 * N, N)


def aligned(v):
    return pl.multiple_of(v, 128)


def mm(a, b, dims):
    return lax.dot_general(a, b, (dims, ((), ())), preferred_element_type=F32)


NN = ((1,), (0,))
NT = ((1,), (1,))
TN = ((0,), (0,))


def route_kernel(
    ids_in, gates_in, tokens, grads, out, pick_out, ids, gates, tok_buf, grad_buf, sems
):
    tok = ids.shape[1]
    small = [
        pltpu.make_async_copy(ids_in, ids, sems.at[4 * N]),
        pltpu.make_async_copy(gates_in, gates, sems.at[4 * N + 1]),
    ]
    for copy in small:
        copy.start()
    copies = []
    for q in range(N):
        for i, (source, buf) in enumerate(((tokens, tok_buf), (grads, grad_buf))):
            for c in range(2):
                cols = pl.ds(c * HALF + q * EIGHTH, EIGHTH)
                copy = pltpu.make_async_copy(
                    source.at[:, cols], buf.at[:, cols], sems.at[q * 4 + i * 2 + c]
                )
                copy.start()
                copies.append(copy)
    row_i = lax.broadcasted_iota(jnp.int32, (tok, tok), 0)
    col_i = lax.broadcasted_iota(jnp.int32, (tok, tok), 1)
    slot = lax.broadcasted_iota(jnp.int32, (ROWS, tok), 0)
    for copy in small:
        copy.wait()
    idv = ids[...]
    gv = gates[...]
    hits = [idv == e for e in range(N)]
    members = [jnp.sum(h.astype(F32), axis=0, keepdims=True) for h in hits]
    chosen = [jnp.sum(jnp.where(h, gv, 0.0), axis=0, keepdims=True) for h in hits]
    mask = jnp.concatenate(members + [jnp.zeros((8 - N, tok), F32)], axis=0)
    before = mm(mask, (row_i < col_i).astype(F32), NN).astype(jnp.int32)
    place_of = jnp.zeros((ROWS, tok), jnp.int32)
    weight = jnp.zeros((ROWS, tok), F32)
    for e in range(N):
        spot = jnp.where(members[e] > 0.0, before[e : e + 1] + e * SLOT, -1)
        mine = slot // SLOT == e
        place_of = jnp.where(mine, spot, place_of)
        weight = jnp.where(mine, chosen[e], weight)
    on = place_of == slot
    pick = jnp.where(on, 1.0, 0.0).astype(BF)
    pick_out[...] = pick
    gate = jnp.sum(jnp.where(on, weight, 0.0), axis=1, keepdims=True)
    for q in range(N):
        for copy in copies[q * 4 : q * 4 + 4]:
            copy.wait()
        for c in range(2):
            cols = slice(c * HALF + q * EIGHTH, c * HALF + (q + 1) * EIGHTH)
            rows = mm(pick, tok_buf[:, cols], NN)
            scaled = mm(pick, grad_buf[:, cols], NN) * gate
            for e in range(N):
                at = slice(e * SLOT, (e + 1) * SLOT)
                both = jnp.concatenate([rows[at], scaled[at]], axis=0).astype(BF)
                out[e * N + q, :, c * EIGHTH : (c + 1) * EIGHTH] = both


def route(ids, gates, tokens, grad_out):
    tok = tokens.shape[0]
    vmem = pl.BlockSpec(memory_space=pltpu.VMEM)
    hbm = pl.BlockSpec(memory_space=pltpu.HBM)
    return pl.pallas_call(
        route_kernel,
        name="route",
        in_specs=[hbm] * 4,
        out_specs=[vmem, vmem],
        out_shape=[
            jax.ShapeDtypeStruct((N * N, 2 * SLOT, QUARTER), BF),
            jax.ShapeDtypeStruct((ROWS, tok), BF),
        ],
        scratch_shapes=[
            pltpu.VMEM(ids.shape, jnp.int32),
            pltpu.VMEM(gates.shape, F32),
            pltpu.VMEM((tok, D), BF),
            pltpu.VMEM((tok, D), BF),
            pltpu.SemaphoreType.DMA((4 * N + 2,)),
        ],
        cost_estimate=pl.CostEstimate(
            flops=4 * ROWS * tok * D, bytes_accessed=6 * tok * D, transcendentals=0
        ),
        compiler_params=pltpu.CompilerParams(vmem_limit_bytes=VMEM_MOST),
    )(ids, gates, tokens, grad_out)


def pair_kernel(place, got, a, b):
    for g in range(N):
        pieces = [got[x * N + g].astype(F32) for x in range(N)]
        for part in range(2):
            rows = [v[part * SLOT : (part + 1) * SLOT] for v in pieces]
            at = (part * 2 + g % 2) * ROWS
            (a, b)[g // 2][at : at + ROWS] = jnp.concatenate(rows, axis=0).astype(BF)


def stack_kernel(place, a0, b0, a1, b3, plus, minus):
    plus[:GROUPED] = a1[...]
    plus[GROUPED:] = b0[...]
    minus[:GROUPED] = b3[...]
    minus[GROUPED:] = a0[...]


def pieces_of(refs):
    if len(refs) == 4:
        a, b, c, d = refs
        return a, b, c, d
    plus, minus = refs
    low, high = pl.ds(0, GROUPED), pl.ds(GROUPED, GROUPED)
    return plus.at[low], minus.at[low], minus.at[high], plus.at[high]


def stack_weights_kernel(place, *refs):
    *pieces, own, other = refs
    y = place[2]
    for out, parts in ((own, pieces[:N]), (other, pieces[N:])):
        for k, w in enumerate(parts):
            block = wrap(y - k)
            for part in range(3):
                rows = pl.ds(pl.multiple_of(part * N * HID + block * HID, HID), HID)
                out[rows, :] = w[part * HID : (part + 1) * HID]


def split_columns_kernel(place, w, o0, o1, o2, o3):
    y = place[2]
    for k, o in enumerate((o0, o1, o2, o3)):
        o[...] = w[0, :, pl.ds(aligned(wrap(y + k) * EIGHTH), EIGHTH)]


def forward_kernel(place, *refs):
    *chunk, own, other, o0, o1, o2, o3, part = refs
    pieces = pieces_of(chunk)
    y, c = place[2], place[3]
    width = N * HID
    mine = pl.ds(aligned(c * EIGHTH), EIGHTH)
    theirs = pl.ds(aligned((1 - c) * EIGHTH), EIGHTH)
    for rows, span in (
        (slice(0, HELD), slice(0, 2 * width)),
        (slice(HELD, 2 * HELD), slice(2 * width, 3 * width)),
    ):
        v_mine = jnp.concatenate([v[rows, mine] for v in pieces], axis=0)
        v_theirs = jnp.concatenate([v[rows, theirs] for v in pieces], axis=0)
        part[:, span] = mm(v_mine, own[span], NT) + mm(v_theirs, other[span], NT)
    for k, o in enumerate((o0, o1, o2, o3)):
        at = wrap(y - k) * ROWS
        for s in range(2):
            rows = pl.ds(pl.multiple_of(s * GROUPED + at, ROWS), ROWS)
            o[s * ROWS : (s + 1) * ROWS] = part[rows, :].astype(o.dtype)


def middle_kernel(place, p0, p1, p2, p3, out):
    width = N * HID
    total = p0[...] + p1[...].astype(F32) + p2[...].astype(F32) + p3[...].astype(F32)
    pair = total[:, : 2 * width]
    d_hidden = total[:, 2 * width :]
    gate = pair[:, :width]
    up = pair[:, width:]
    sig = jax.nn.sigmoid(gate)
    act = gate * sig
    out[:, :width] = (d_hidden * up * sig * (1.0 + gate * (1.0 - sig))).astype(BF)
    out[:, width : 2 * width] = (d_hidden * act).astype(BF)
    out[:, 2 * width :] = (act * up).astype(BF)


def back_kernel(place, held, own, other, *outs):
    c = place[3]
    width = 2 * N * HID
    h = held[:, :width]
    if len(outs) == 2:
        minus, plus = outs
        targets = (minus, 0), (plus, 0), (plus, HELD), (minus, HELD)
    else:
        targets = [(o, 0) for o in outs]
    for w, half in ((own, c), (other, 1 - c)):
        cols = pl.ds(aligned(half * EIGHTH), EIGHTH)
        part = mm(h, w[:width], NN)
        for i, (o, at) in enumerate(targets):
            o[at : at + HELD, cols] = part[i * HELD : (i + 1) * HELD].astype(BF)


def pass_on_kernel(place, own_a, own_b, got_a, got_b, out_a, out_b):
    out_a[...] = (own_a[...].astype(F32) + got_a[:HELD].astype(F32)).astype(BF)
    out_b[...] = (own_b[...].astype(F32) + got_b[:HELD].astype(F32)).astype(BF)


def weight_grad(half, held, chunk, add):
    pieces = pieces_of(chunk)
    width = 2 * N * HID
    cols = pl.ds(aligned(half * EIGHTH), EIGHTH)
    x = jnp.concatenate([v[:HELD, cols] for v in pieces], axis=0)
    add(slice(0, width), mm(held[:, :width], x, TN))
    g = jnp.concatenate([v[HELD : 2 * HELD, cols] for v in pieces], axis=0)
    add(slice(width, 3 * N * HID), mm(held[:, width:], g, TN))


def assemble(y, parts, held):
    for k, h in enumerate(parts):
        at = wrap(y - k) * ROWS
        for s in range(2):
            rows = pl.ds(pl.multiple_of(s * GROUPED + at, ROWS), ROWS)
            held[rows, :] = h[s * ROWS : (s + 1) * ROWS]


def first_grad_kernel(place, *refs):
    *chunk, held, theirs, mine = refs[N:]
    assemble(place[2], refs[:N], held)
    for out, half in ((theirs, 1 - place[3]), (mine, place[3])):

        def add(rows, value, out=out):
            out[rows] = value

        weight_grad(half, held, chunk, add)


def their_grad_kernel(place, *refs):
    before, plus, minus, held, o0, o1, o2 = refs[N:]
    assemble(place[2], refs[:N], held)

    def add(rows, value):
        total = (value + before[rows]).astype(BF)
        for i, o in enumerate((o0, o1, o2)):
            at = i * N * HID - rows.start
            if 0 <= at < total.shape[0]:
                o[...] = total[at : at + N * HID]

    weight_grad(1 - place[3], held, (plus, minus), add)


def my_grad_kernel(place, got0, got1, got2, held, before, plus, minus, o0, o1, o2, o3, mine):
    y = place[2]

    def add(rows, value):
        mine[rows] = value + before[rows]

    weight_grad(place[3], held, (plus, minus), add)
    for k, o in enumerate((o0, o1, o2, o3)):
        block = pl.multiple_of(wrap(y - k) * HID, HID)
        for part, got in enumerate((got0, got1, got2)):
            own = mine[pl.ds(pl.multiple_of(part * N * HID + block, HID), HID), :]
            total = own + got[pl.ds(block, HID), :].astype(F32)
            o[part * HID : (part + 1) * HID] = total.astype(o.dtype)


def sum_back_kernel(place, a0, b0, a1, b3, got_minus, got_plus, out):
    for h, (i, j, k) in enumerate(((a0, a1, got_plus), (b0, b3, got_minus))):
        total = i[...].astype(F32) + (j[...].astype(F32) + k[HELD:].astype(F32))
        for s in range(2):
            for x in range(N):
                at = s * ROWS + x * SLOT
                out[x * N + 2 * h + s] = total[at : at + SLOT].astype(BF)


def combine_kernel(place, pick, got, out, sums, sems):
    copies = []
    for q in range(N):
        rows = jnp.concatenate([got[e * N + q].astype(F32) for e in range(N)], axis=0)
        sums[q] = mm(pick[...], rows.astype(BF), TN).astype(BF)
        for c in range(2):
            copy = pltpu.make_async_copy(
                sums.at[q, :, pl.ds(c * EIGHTH, EIGHTH)],
                out.at[:, pl.ds(c * HALF + q * EIGHTH, EIGHTH)],
                sems.at[q * 2 + c],
            )
            copy.start()
            copies.append(copy)
    for copy in copies:
        copy.wait()


def moments_kernel(place, g0, g1, g2, g3, one, two, new_one, new_two):
    step = pl.program_id(0)
    for k, g in enumerate((g0, g1, g2, g3)):

        @pl.when(step == k)
        def _():
            grad = g[...].astype(F32)
            new_one[0] = beta_one * one[0] + (1.0 - beta_one) * grad
            new_two[0] = beta_two * two[0] + (1.0 - beta_two) * grad * grad


def moments(place, grads, one, two):
    rows = one.shape[1]
    piece = pl.BlockSpec((rows, EIGHTH), lambda k, place: (0, 0))
    block = pl.BlockSpec((1, rows, EIGHTH), lambda k, place: (0, 0, lax.rem(place[2] + k, N)))
    return pl.pallas_call(
        moments_kernel,
        name="moments",
        grid_spec=pltpu.PrefetchScalarGridSpec(
            num_scalar_prefetch=1,
            grid=(N,),
            in_specs=[piece] * N + [block] * 2,
            out_specs=[block] * 2,
        ),
        out_shape=[jax.ShapeDtypeStruct(v.shape, v.dtype) for v in (one, two)],
        cost_estimate=pl.CostEstimate(
            flops=6 * one.size, bytes_accessed=17 * one.size, transcendentals=0
        ),
        compiler_params=pltpu.CompilerParams(vmem_limit_bytes=VMEM_MOST),
    )(place, *grads, one, two)


def exchange(value, axes):
    groups = {}
    for index in range(N * N * N):
        at = {"x": index // (N * N), "z": index // N % N, "y": index % N}
        groups.setdefault(tuple(at[a] for a in at if a not in axes), []).append(index)
    return lax.all_to_all(
        value, "expert", 0, 0, axis_index_groups=list(groups.values()), tiled=True
    )


def spread(parts, axis, sign=1):
    moved = {k: turn(parts[k], axis, sign * k) for k in (2, 1, 3)}
    return [parts[0]] + [moved[k] for k in range(1, N)]


def after(values, *earlier):
    return lax.optimization_barrier((values, earlier))[0]


def pass_on(place, *parts):
    half = ((HELD, QUARTER), BF)
    return call(pass_on_kernel, "pass_on", [half] * 2, place, *parts)


def forward_part(place, chunk, w_own, w_other):
    width = 3 * N * HID
    return call(
        forward_kernel,
        "forward",
        [((HELD, width), F32)] + [((HELD, width), BF)] * 3,
        place,
        *chunk,
        w_own,
        w_other,
        flops=2 * CHUNK * QUARTER * width,
        scratch=[pltpu.VMEM((CHUNK, width), F32)],
    )


def middle_part(place, part):
    return call(middle_kernel, "middle", [((HELD, 3 * N * HID), BF)], place, *part)[0]


def back_part(place, held, w_own, w_other, chunk):
    shape = (HELD, QUARTER) if chunk == 0 else (2 * HELD, QUARTER)
    return call(
        back_kernel,
        "back",
        [(shape, BF)] * (CHUNK // shape[0]),
        place,
        held,
        w_own,
        w_other,
        flops=4 * CHUNK * QUARTER * N * HID,
    )


def shards(tokens, grad_out, gates, expert_ids, expert_weights, moment_one, moment_two):
    expert = lax.axis_index("expert")
    core = lax.axis_index("dp")
    place = jnp.stack([expert // (N * N), expert // N % N, expert % N, core]).astype(jnp.int32)
    tok = tokens.shape[0]
    width = N * HID
    slots = ((N * N, SLOT, QUARTER), BF)
    block_rows = expert_weights.shape[1]

    sent, pick = route(expert_ids.T, gates.T, tokens, grad_out)
    got = exchange(sent, "xy")
    w_columns = call(
        split_columns_kernel,
        "split_columns",
        [((block_rows, EIGHTH), BF)] * N,
        place,
        expert_weights,
    )
    w_parts = spread(w_columns, "y")
    got = after(got, w_columns[1])
    a0, b0 = call(pair_kernel, "pair", [((GROUPED, QUARTER), BF)] * 2, place, got)
    a1, b3 = turn(a0, "z", 1), turn(b0, "z", -1)
    first = a0, b0, a1, b3
    plus, minus = call(
        stack_kernel, "stack", [((2 * GROUPED, QUARTER), BF)] * 2, place, *first
    )
    w_parts = after(w_parts, plus)
    second = turn(plus, "z", 1), turn(minus, "z", -1)
    w_others = [turn(w, "c", 1) for w in w_parts]
    w_own, w_other = call(
        stack_weights_kernel,
        "stack_weights",
        [((N * block_rows, EIGHTH), BF)] * 2,
        place,
        *w_parts,
        *w_others,
    )

    part_one = forward_part(place, first, w_own, w_other)
    part_one = spread(part_one, "y", -1)
    part_two = forward_part(place, second, w_own, w_other)
    part_one = after(part_one, part_two[1])
    part_two = spread(part_two, "y", -1)
    mid_one = middle_part(place, part_one)
    held_one = spread([mid_one] * N, "y")
    mid_two = middle_part(place, part_two)
    held_two = spread([mid_two] * N, "y")
    flops = N * GROUPED * QUARTER * 3 * width
    held_one, first_theirs, first_mine = call(
        first_grad_kernel,
        "first_grad",
        [((CHUNK, 3 * width), BF)] + [((3 * width, EIGHTH), F32)] * 2,
        place,
        *held_one,
        *first,
        flops=flops,
    )
    held_two, *theirs = call(
        their_grad_kernel,
        "their_grad",
        [((CHUNK, 3 * width), BF)] + [((width, EIGHTH), BF)] * 3,
        place,
        *held_two,
        first_theirs,
        *second,
        flops=flops // 2,
    )
    minus, plus = back_part(place, held_two, w_own, w_other, 1)
    got_minus, got_plus = turn(minus, "z", -1), turn(plus, "z", 1)
    got = [turn(v, "c", 1) for v in theirs]
    blocks = call(
        my_grad_kernel,
        "my_grad",
        [((block_rows, EIGHTH), F32)] + [((block_rows, EIGHTH), BF)] * 3,
        place,
        *got,
        after(held_two, minus),
        first_mine,
        *second,
        flops=flops // 2,
        scratch=[pltpu.VMEM((3 * width, EIGHTH), F32)],
    )
    a0, b0, a1, b3 = back_part(place, after(held_one, blocks[0]), w_own, w_other, 0)
    a1, b3 = pass_on(place, *after((a1, b3, got_minus, got_plus), blocks[0]))
    a1, b3 = turn(a1, "z", -1), turn(b3, "z", 1)
    blocks = spread(blocks, "y", -1)
    parts = after((a0, b0, a1, b3, got_minus, got_plus), *blocks)
    (back,) = call(sum_back_kernel, "sum_back", [slots], place, *parts)
    back = exchange(back, "xy")
    new_one, new_two = moments(place, blocks, moment_one, moment_two)
    back = after(back, new_one)
    (grad_tokens,) = call(
        combine_kernel,
        "combine",
        [((tok, D), BF)],
        place,
        pick,
        back,
        flops=2 * ROWS * tok * D,
        scratch=[pltpu.VMEM((N, tok, QUARTER), BF), pltpu.SemaphoreType.DMA((2 * N,))],
        own_copies=(0,),
    )
    return grad_tokens, new_one, new_two


def solution(mesh):
    return jax.shard_map(
        shards,
        mesh=mesh,
        in_specs=(
            P(("expert", "dp"), None),
            P(("expert", "dp"), None),
            P(("expert", "dp"), None),
            P(("expert", "dp"), None),
            P("expert", None, "dp"),
            P("expert", None, "dp"),
            P("expert", None, "dp"),
        ),
        out_specs=(P(("expert", "dp"), None), P("expert", None, "dp"), P("expert", None, "dp")),
        check_vma=False,
    )
```

```python
import functools

import jax
import jax.numpy as jnp
from jax import lax
from jax.experimental import pallas as pl
from jax.experimental.pallas import tpu as pltpu
from jax.sharding import PartitionSpec as P

N = 4
SLOT = 8
HID = 64
D = 7168
HALF = D // 2
EIGHTH = HALF // N
QUARTER = 2 * EIGHTH
ROWS = N * SLOT
GROUPED = N * ROWS
HELD = 2 * ROWS
CHUNK = N * HELD
BF = jnp.bfloat16
F32 = jnp.float32
VMEM_LIMIT = 16 * 1024 * 1024
VMEM_MOST = 56 * 1024 * 1024
beta_one = 0.9
beta_two = 0.95


def rotation(axis, step):
    pairs = []
    for x in range(N):
        for z in range(N):
            for y in range(N):
                for c in range(2):
                    to = {"x": x, "z": z, "y": y, "c": c}
                    to[axis] = (to[axis] + step) % (2 if axis == "c" else N)
                    source = ((x * N + z) * N + y) * 2 + c
                    target = ((to["x"] * N + to["z"]) * N + to["y"]) * 2 + to["c"]
                    pairs.append((source, target))
    return pairs


def turn(value, axis, step):
    return lax.ppermute(value, ("expert", "dp"), rotation(axis, step))


def call(kernel, name, outs, place, *ins, flops=0, scratch=(), own_copies=()):
    outs = [jax.ShapeDtypeStruct(s, t) for s, t in outs]
    size = sum(v.size * v.dtype.itemsize for v in (*ins, *outs))
    return pl.pallas_call(
        kernel,
        name=name,
        out_shape=outs,
        in_specs=[pl.BlockSpec(memory_space=pltpu.SMEM)]
        + [pl.BlockSpec(memory_space=pltpu.VMEM)] * len(ins),
        out_specs=[
            pl.BlockSpec(memory_space=pl.ANY if i in own_copies else pltpu.VMEM)
            for i in range(len(outs))
        ],
        scratch_shapes=list(scratch),
        cost_estimate=pl.CostEstimate(flops=flops, bytes_accessed=size, transcendentals=0),
        compiler_params=pltpu.CompilerParams(vmem_limit_bytes=VMEM_LIMIT),
    )(place, *ins)


def wrap(v):
    return lax.rem(v + 2 * N, N)


def aligned(v):
    return pl.multiple_of(v, 128)


def mm(a, b, dims):
    return lax.dot_general(a, b, (dims, ((), ())), preferred_element_type=F32)


NN = ((1,), (0,))
NT = ((1,), (1,))
TN = ((0,), (0,))


def route_kernel(
    ids_in, gates_in, tokens, grads, out, pick_out, ids, gates, tok_buf, grad_buf, sems
):
    tok = ids.shape[1]
    small = [
        pltpu.make_async_copy(ids_in, ids, sems.at[4 * N]),
        pltpu.make_async_copy(gates_in, gates, sems.at[4 * N + 1]),
    ]
    for copy in small:
        copy.start()
    copies = []
    for q in range(N):
        for i, (source, buf) in enumerate(((tokens, tok_buf), (grads, grad_buf))):
            for c in range(2):
                cols = pl.ds(c * HALF + q * EIGHTH, EIGHTH)
                copy = pltpu.make_async_copy(
                    source.at[:, cols], buf.at[:, cols], sems.at[q * 4 + i * 2 + c]
                )
                copy.start()
                copies.append(copy)
    row_i = lax.broadcasted_iota(jnp.int32, (tok, tok), 0)
    col_i = lax.broadcasted_iota(jnp.int32, (tok, tok), 1)
    slot = lax.broadcasted_iota(jnp.int32, (ROWS, tok), 0)
    for copy in small:
        copy.wait()
    idv = ids[...]
    gv = gates[...]
    hits = [idv == e for e in range(N)]
    members = [jnp.sum(h.astype(F32), axis=0, keepdims=True) for h in hits]
    chosen = [jnp.sum(jnp.where(h, gv, 0.0), axis=0, keepdims=True) for h in hits]
    mask = jnp.concatenate(members + [jnp.zeros((8 - N, tok), F32)], axis=0)
    before = mm(mask, (row_i < col_i).astype(F32), NN).astype(jnp.int32)
    place_of = jnp.zeros((ROWS, tok), jnp.int32)
    weight = jnp.zeros((ROWS, tok), F32)
    for e in range(N):
        spot = jnp.where(members[e] > 0.0, before[e : e + 1] + e * SLOT, -1)
        mine = slot // SLOT == e
        place_of = jnp.where(mine, spot, place_of)
        weight = jnp.where(mine, chosen[e], weight)
    on = place_of == slot
    pick = jnp.where(on, 1.0, 0.0).astype(BF)
    pick_out[...] = pick
    gate = jnp.sum(jnp.where(on, weight, 0.0), axis=1, keepdims=True)
    for q in range(N):
        for copy in copies[q * 4 : q * 4 + 4]:
            copy.wait()
        for c in range(2):
            cols = slice(c * HALF + q * EIGHTH, c * HALF + (q + 1) * EIGHTH)
            rows = mm(pick, tok_buf[:, cols], NN)
            scaled = mm(pick, grad_buf[:, cols], NN) * gate
            for e in range(N):
                at = slice(e * SLOT, (e + 1) * SLOT)
                both = jnp.concatenate([rows[at], scaled[at]], axis=0).astype(BF)
                out[e * N + q, :, c * EIGHTH : (c + 1) * EIGHTH] = both


def route(ids, gates, tokens, grad_out):
    tok = tokens.shape[0]
    vmem = pl.BlockSpec(memory_space=pltpu.VMEM)
    hbm = pl.BlockSpec(memory_space=pltpu.HBM)
    return pl.pallas_call(
        route_kernel,
        name="route",
        in_specs=[hbm] * 4,
        out_specs=[vmem, vmem],
        out_shape=[
            jax.ShapeDtypeStruct((N * N, 2 * SLOT, QUARTER), BF),
            jax.ShapeDtypeStruct((ROWS, tok), BF),
        ],
        scratch_shapes=[
            pltpu.VMEM(ids.shape, jnp.int32),
            pltpu.VMEM(gates.shape, F32),
            pltpu.VMEM((tok, D), BF),
            pltpu.VMEM((tok, D), BF),
            pltpu.SemaphoreType.DMA((4 * N + 2,)),
        ],
        cost_estimate=pl.CostEstimate(
            flops=4 * ROWS * tok * D, bytes_accessed=6 * tok * D, transcendentals=0
        ),
        compiler_params=pltpu.CompilerParams(vmem_limit_bytes=VMEM_MOST),
    )(ids, gates, tokens, grad_out)


def pair_kernel(place, got, a, b):
    for g in range(N):
        pieces = [got[x * N + g].astype(F32) for x in range(N)]
        for part in range(2):
            rows = [v[part * SLOT : (part + 1) * SLOT] for v in pieces]
            at = (part * 2 + g % 2) * ROWS
            (a, b)[g // 2][at : at + ROWS] = jnp.concatenate(rows, axis=0).astype(BF)


def stack_kernel(place, a0, b0, a1, b3, plus, minus):
    plus[:GROUPED] = a1[...]
    plus[GROUPED:] = b0[...]
    minus[:GROUPED] = b3[...]
    minus[GROUPED:] = a0[...]


def pieces_of(refs):
    if len(refs) == 4:
        a, b, c, d = refs
        return a, b, c, d
    plus, minus = refs
    low, high = pl.ds(0, GROUPED), pl.ds(GROUPED, GROUPED)
    return plus.at[low], minus.at[low], minus.at[high], plus.at[high]


def stack_weights_kernel(place, *refs):
    *pieces, own, other = refs
    y = place[2]
    for out, parts in ((own, pieces[:N]), (other, pieces[N:])):
        for k, w in enumerate(parts):
            block = wrap(y - k)
            for part in range(3):
                rows = pl.ds(pl.multiple_of(part * N * HID + block * HID, HID), HID)
                out[rows, :] = w[part * HID : (part + 1) * HID]


def split_columns_kernel(place, w, o0, o1, o2, o3):
    y = place[2]
    for k, o in enumerate((o0, o1, o2, o3)):
        o[...] = w[0, :, pl.ds(aligned(wrap(y + k) * EIGHTH), EIGHTH)]


def forward_kernel(place, *refs):
    *chunk, own, other, o0, o1, o2, o3, part = refs
    pieces = pieces_of(chunk)
    y, c = place[2], place[3]
    width = N * HID
    mine = pl.ds(aligned(c * EIGHTH), EIGHTH)
    theirs = pl.ds(aligned((1 - c) * EIGHTH), EIGHTH)
    for rows, span in (
        (slice(0, HELD), slice(0, 2 * width)),
        (slice(HELD, 2 * HELD), slice(2 * width, 3 * width)),
    ):
        v_mine = jnp.concatenate([v[rows, mine] for v in pieces], axis=0)
        v_theirs = jnp.concatenate([v[rows, theirs] for v in pieces], axis=0)
        part[:, span] = mm(v_mine, own[span], NT) + mm(v_theirs, other[span], NT)
    for k, o in enumerate((o0, o1, o2, o3)):
        at = wrap(y - k) * ROWS
        for s in range(2):
            rows = pl.ds(pl.multiple_of(s * GROUPED + at, ROWS), ROWS)
            o[s * ROWS : (s + 1) * ROWS] = part[rows, :].astype(o.dtype)


def middle_kernel(place, p0, p1, p2, p3, out):
    width = N * HID
    total = p0[...] + p1[...].astype(F32) + p2[...].astype(F32) + p3[...].astype(F32)
    pair = total[:, : 2 * width]
    d_hidden = total[:, 2 * width :]
    gate = pair[:, :width]
    up = pair[:, width:]
    sig = jax.nn.sigmoid(gate)
    act = gate * sig
    out[:, :width] = (d_hidden * up * sig * (1.0 + gate * (1.0 - sig))).astype(BF)
    out[:, width : 2 * width] = (d_hidden * act).astype(BF)
    out[:, 2 * width :] = (act * up).astype(BF)


def back_kernel(place, held, own, other, *outs):
    c = place[3]
    width = 2 * N * HID
    h = held[:, :width]
    if len(outs) == 2:
        minus, plus = outs
        targets = (minus, 0), (plus, 0), (plus, HELD), (minus, HELD)
    else:
        targets = [(o, 0) for o in outs]
    for w, half in ((own, c), (other, 1 - c)):
        cols = pl.ds(aligned(half * EIGHTH), EIGHTH)
        part = mm(h, w[:width], NN)
        for i, (o, at) in enumerate(targets):
            o[at : at + HELD, cols] = part[i * HELD : (i + 1) * HELD].astype(BF)


def pass_on_kernel(place, own_a, own_b, got_a, got_b, out_a, out_b):
    out_a[...] = (own_a[...].astype(F32) + got_a[:HELD].astype(F32)).astype(BF)
    out_b[...] = (own_b[...].astype(F32) + got_b[:HELD].astype(F32)).astype(BF)


def weight_grad(half, held, chunk, add):
    pieces = pieces_of(chunk)
    width = 2 * N * HID
    cols = pl.ds(aligned(half * EIGHTH), EIGHTH)
    x = jnp.concatenate([v[:HELD, cols] for v in pieces], axis=0)
    add(slice(0, width), mm(held[:, :width], x, TN))
    g = jnp.concatenate([v[HELD : 2 * HELD, cols] for v in pieces], axis=0)
    add(slice(width, 3 * N * HID), mm(held[:, width:], g, TN))


def assemble(y, parts, held):
    for k, h in enumerate(parts):
        at = wrap(y - k) * ROWS
        for s in range(2):
            rows = pl.ds(pl.multiple_of(s * GROUPED + at, ROWS), ROWS)
            held[rows, :] = h[s * ROWS : (s + 1) * ROWS]


def first_grad_kernel(place, *refs):
    *chunk, held, theirs, mine = refs[N:]
    assemble(place[2], refs[:N], held)
    for out, half in ((theirs, 1 - place[3]), (mine, place[3])):

        def add(rows, value, out=out):
            out[rows] = value

        weight_grad(half, held, chunk, add)


def their_grad_kernel(place, *refs):
    before, plus, minus, held, out = refs[N:]
    assemble(place[2], refs[:N], held)

    def add(rows, value):
        out[rows] = (value + before[rows]).astype(BF)

    weight_grad(1 - place[3], held, (plus, minus), add)


def my_grad_kernel(place, got, held, before, plus, minus, o0, o1, o2, o3, mine):
    y = place[2]

    def add(rows, value):
        mine[rows] = value + before[rows]

    weight_grad(place[3], held, (plus, minus), add)
    for k, o in enumerate((o0, o1, o2, o3)):
        block = pl.multiple_of(wrap(y - k) * HID, HID)
        for part in range(3):
            rows = pl.ds(pl.multiple_of(part * N * HID + block, HID), HID)
            total = mine[rows, :] + got[rows, :].astype(F32)
            o[part * HID : (part + 1) * HID] = total.astype(o.dtype)


def sum_back_kernel(place, a0, b0, a1, b3, got_minus, got_plus, out):
    for h, (i, j, k) in enumerate(((a0, a1, got_plus), (b0, b3, got_minus))):
        total = i[...].astype(F32) + (j[...].astype(F32) + k[HELD:].astype(F32))
        for s in range(2):
            for x in range(N):
                at = s * ROWS + x * SLOT
                out[x * N + 2 * h + s] = total[at : at + SLOT].astype(BF)


def combine_kernel(place, pick, got, out, sums, sems):
    copies = []
    for q in range(N):
        rows = jnp.concatenate([got[e * N + q].astype(F32) for e in range(N)], axis=0)
        sums[q] = mm(pick[...], rows.astype(BF), TN).astype(BF)
        for c in range(2):
            copy = pltpu.make_async_copy(
                sums.at[q, :, pl.ds(c * EIGHTH, EIGHTH)],
                out.at[:, pl.ds(c * HALF + q * EIGHTH, EIGHTH)],
                sems.at[q * 2 + c],
            )
            copy.start()
            copies.append(copy)
    for copy in copies:
        copy.wait()


def moments_kernel(place, g0, g1, g2, g3, one, two, new_one, new_two):
    step = pl.program_id(0)
    for k, g in enumerate((g0, g1, g2, g3)):

        @pl.when(step == k)
        def _():
            grad = g[...].astype(F32)
            new_one[0] = beta_one * one[0] + (1.0 - beta_one) * grad
            new_two[0] = beta_two * two[0] + (1.0 - beta_two) * grad * grad


def moments(place, grads, one, two):
    rows = one.shape[1]
    piece = pl.BlockSpec((rows, EIGHTH), lambda k, place: (0, 0))
    block = pl.BlockSpec((1, rows, EIGHTH), lambda k, place: (0, 0, lax.rem(place[2] + k, N)))
    return pl.pallas_call(
        moments_kernel,
        name="moments",
        grid_spec=pltpu.PrefetchScalarGridSpec(
            num_scalar_prefetch=1,
            grid=(N,),
            in_specs=[piece] * N + [block] * 2,
            out_specs=[block] * 2,
        ),
        out_shape=[jax.ShapeDtypeStruct(v.shape, v.dtype) for v in (one, two)],
        cost_estimate=pl.CostEstimate(
            flops=6 * one.size, bytes_accessed=17 * one.size, transcendentals=0
        ),
        compiler_params=pltpu.CompilerParams(vmem_limit_bytes=VMEM_MOST),
    )(place, *grads, one, two)


def exchange(value, axes):
    groups = {}
    for index in range(N * N * N):
        at = {"x": index // (N * N), "z": index // N % N, "y": index % N}
        groups.setdefault(tuple(at[a] for a in at if a not in axes), []).append(index)
    return lax.all_to_all(
        value, "expert", 0, 0, axis_index_groups=list(groups.values()), tiled=True
    )


def spread(parts, axis, sign=1):
    moved = {k: turn(parts[k], axis, sign * k) for k in (2, 1, 3)}
    return [parts[0]] + [moved[k] for k in range(1, N)]


def after(values, *earlier):
    return lax.optimization_barrier((values, earlier))[0]


def pass_on(place, *parts):
    half = ((HELD, QUARTER), BF)
    return call(pass_on_kernel, "pass_on", [half] * 2, place, *parts)


def forward_part(place, chunk, w_own, w_other):
    width = 3 * N * HID
    return call(
        forward_kernel,
        "forward",
        [((HELD, width), F32)] + [((HELD, width), BF)] * 3,
        place,
        *chunk,
        w_own,
        w_other,
        flops=2 * CHUNK * QUARTER * width,
        scratch=[pltpu.VMEM((CHUNK, width), F32)],
    )


def middle_part(place, part):
    return call(middle_kernel, "middle", [((HELD, 3 * N * HID), BF)], place, *part)[0]


def back_part(place, held, w_own, w_other, chunk):
    shape = (HELD, QUARTER) if chunk == 0 else (2 * HELD, QUARTER)
    return call(
        back_kernel,
        "back",
        [(shape, BF)] * (CHUNK // shape[0]),
        place,
        held,
        w_own,
        w_other,
        flops=4 * CHUNK * QUARTER * N * HID,
    )


def shards(tokens, grad_out, gates, expert_ids, expert_weights, moment_one, moment_two):
    expert = lax.axis_index("expert")
    core = lax.axis_index("dp")
    place = jnp.stack([expert // (N * N), expert // N % N, expert % N, core]).astype(jnp.int32)
    tok = tokens.shape[0]
    width = N * HID
    slots = ((N * N, SLOT, QUARTER), BF)
    block_rows = expert_weights.shape[1]

    sent, pick = route(expert_ids.T, gates.T, tokens, grad_out)
    got = exchange(sent, "xy")
    w_columns = call(
        split_columns_kernel,
        "split_columns",
        [((block_rows, EIGHTH), BF)] * N,
        place,
        expert_weights,
    )
    w_parts = spread(w_columns, "y")
    got = after(got, w_columns[1])
    a0, b0 = call(pair_kernel, "pair", [((GROUPED, QUARTER), BF)] * 2, place, got)
    a1, b3 = turn(a0, "z", 1), turn(b0, "z", -1)
    first = a0, b0, a1, b3
    plus, minus = call(
        stack_kernel, "stack", [((2 * GROUPED, QUARTER), BF)] * 2, place, *first
    )
    w_parts = after(w_parts, plus)
    second = turn(plus, "z", 1), turn(minus, "z", -1)
    w_others = [turn(w, "c", 1) for w in w_parts]
    w_own, w_other = call(
        stack_weights_kernel,
        "stack_weights",
        [((N * block_rows, EIGHTH), BF)] * 2,
        place,
        *w_parts,
        *w_others,
    )

    part_one = forward_part(place, first, w_own, w_other)
    part_one = spread(part_one, "y", -1)
    part_two = forward_part(place, second, w_own, w_other)
    part_one = after(part_one, part_two[1])
    part_two = spread(part_two, "y", -1)
    mid_one = middle_part(place, part_one)
    held_one = spread([mid_one] * N, "y")
    mid_two = middle_part(place, part_two)
    held_two = spread([mid_two] * N, "y")
    flops = N * GROUPED * QUARTER * 3 * width
    held_one, first_theirs, first_mine = call(
        first_grad_kernel,
        "first_grad",
        [((CHUNK, 3 * width), BF)] + [((3 * width, EIGHTH), F32)] * 2,
        place,
        *held_one,
        *first,
        flops=flops,
    )
    held_two, theirs = call(
        their_grad_kernel,
        "their_grad",
        [((CHUNK, 3 * width), BF), ((3 * width, EIGHTH), BF)],
        place,
        *held_two,
        first_theirs,
        *second,
        flops=flops // 2,
    )
    minus, plus = back_part(place, held_two, w_own, w_other, 1)
    got_minus, got_plus = turn(minus, "z", -1), turn(plus, "z", 1)
    got = turn(theirs, "c", 1)
    blocks = call(
        my_grad_kernel,
        "my_grad",
        [((block_rows, EIGHTH), F32)] + [((block_rows, EIGHTH), BF)] * 3,
        place,
        got,
        after(held_two, minus),
        first_mine,
        *second,
        flops=flops // 2,
        scratch=[pltpu.VMEM((3 * width, EIGHTH), F32)],
    )
    a0, b0, a1, b3 = back_part(place, after(held_one, blocks[0]), w_own, w_other, 0)
    a1, b3 = pass_on(place, *after((a1, b3, got_minus, got_plus), blocks[0]))
    a1, b3 = turn(a1, "z", -1), turn(b3, "z", 1)
    blocks = spread(blocks, "y", -1)
    parts = after((a0, b0, a1, b3, got_minus, got_plus), *blocks)
    (back,) = call(sum_back_kernel, "sum_back", [slots], place, *parts)
    back = exchange(back, "xy")
    new_one, new_two = moments(place, blocks, moment_one, moment_two)
    back = after(back, new_one)
    (grad_tokens,) = call(
        combine_kernel,
        "combine",
        [((tok, D), BF)],
        place,
        pick,
        back,
        flops=2 * ROWS * tok * D,
        scratch=[pltpu.VMEM((N, tok, QUARTER), BF), pltpu.SemaphoreType.DMA((2 * N,))],
        own_copies=(0,),
    )
    return grad_tokens, new_one, new_two


def solution(mesh):
    return jax.shard_map(
        shards,
        mesh=mesh,
        in_specs=(
            P(("expert", "dp"), None),
            P(("expert", "dp"), None),
            P(("expert", "dp"), None),
            P(("expert", "dp"), None),
            P("expert", None, "dp"),
            P("expert", None, "dp"),
            P("expert", None, "dp"),
        ),
        out_specs=(P(("expert", "dp"), None), P("expert", None, "dp"), P("expert", None, "dp")),
        check_vma=False,
    )
```

```python
import functools

import jax
import jax.numpy as jnp
from jax import lax
from jax.experimental import pallas as pl
from jax.experimental.pallas import tpu as pltpu
from jax.sharding import PartitionSpec as P

N = 4
SLOT = 8
HID = 64
D = 7168
HALF = D // 2
EIGHTH = HALF // N
QUARTER = 2 * EIGHTH
ROWS = N * SLOT
GROUPED = N * ROWS
HELD = 2 * ROWS
CHUNK = N * HELD
BF = jnp.bfloat16
F32 = jnp.float32
VMEM_LIMIT = 16 * 1024 * 1024
VMEM_MOST = 56 * 1024 * 1024
beta_one = 0.9
beta_two = 0.95


def rotation(axis, step):
    pairs = []
    for x in range(N):
        for z in range(N):
            for y in range(N):
                for c in range(2):
                    to = {"x": x, "z": z, "y": y, "c": c}
                    to[axis] = (to[axis] + step) % (2 if axis == "c" else N)
                    source = ((x * N + z) * N + y) * 2 + c
                    target = ((to["x"] * N + to["z"]) * N + to["y"]) * 2 + to["c"]
                    pairs.append((source, target))
    return pairs


def turn(value, axis, step):
    return lax.ppermute(value, ("expert", "dp"), rotation(axis, step))


def call(kernel, name, outs, place, *ins, flops=0, scratch=(), own_copies=()):
    outs = [jax.ShapeDtypeStruct(s, t) for s, t in outs]
    size = sum(v.size * v.dtype.itemsize for v in (*ins, *outs))
    return pl.pallas_call(
        kernel,
        name=name,
        out_shape=outs,
        in_specs=[pl.BlockSpec(memory_space=pltpu.SMEM)]
        + [pl.BlockSpec(memory_space=pltpu.VMEM)] * len(ins),
        out_specs=[
            pl.BlockSpec(memory_space=pl.ANY if i in own_copies else pltpu.VMEM)
            for i in range(len(outs))
        ],
        scratch_shapes=list(scratch),
        cost_estimate=pl.CostEstimate(flops=flops, bytes_accessed=size, transcendentals=0),
        compiler_params=pltpu.CompilerParams(vmem_limit_bytes=VMEM_LIMIT),
    )(place, *ins)


def wrap(v):
    return lax.rem(v + 2 * N, N)


def aligned(v):
    return pl.multiple_of(v, 128)


def mm(a, b, dims):
    return lax.dot_general(a, b, (dims, ((), ())), preferred_element_type=F32)


NN = ((1,), (0,))
NT = ((1,), (1,))
TN = ((0,), (0,))


def route_kernel(
    ids_in, gates_in, tokens, grads, out, pick_out, ids, gates, tok_buf, grad_buf, sems
):
    tok = ids.shape[1]
    small = [
        pltpu.make_async_copy(ids_in, ids, sems.at[4 * N]),
        pltpu.make_async_copy(gates_in, gates, sems.at[4 * N + 1]),
    ]
    for copy in small:
        copy.start()
    copies = []
    for q in range(N):
        for i, (source, buf) in enumerate(((tokens, tok_buf), (grads, grad_buf))):
            for c in range(2):
                cols = pl.ds(c * HALF + q * EIGHTH, EIGHTH)
                copy = pltpu.make_async_copy(
                    source.at[:, cols], buf.at[:, cols], sems.at[q * 4 + i * 2 + c]
                )
                copy.start()
                copies.append(copy)
    row_i = lax.broadcasted_iota(jnp.int32, (tok, tok), 0)
    col_i = lax.broadcasted_iota(jnp.int32, (tok, tok), 1)
    slot = lax.broadcasted_iota(jnp.int32, (ROWS, tok), 0)
    for copy in small:
        copy.wait()
    idv = ids[...]
    gv = gates[...]
    hits = [idv == e for e in range(N)]
    members = [jnp.sum(h.astype(F32), axis=0, keepdims=True) for h in hits]
    chosen = [jnp.sum(jnp.where(h, gv, 0.0), axis=0, keepdims=True) for h in hits]
    mask = jnp.concatenate(members + [jnp.zeros((8 - N, tok), F32)], axis=0)
    before = mm(mask, (row_i < col_i).astype(F32), NN).astype(jnp.int32)
    place_of = jnp.zeros((ROWS, tok), jnp.int32)
    weight = jnp.zeros((ROWS, tok), F32)
    for e in range(N):
        spot = jnp.where(members[e] > 0.0, before[e : e + 1] + e * SLOT, -1)
        mine = slot // SLOT == e
        place_of = jnp.where(mine, spot, place_of)
        weight = jnp.where(mine, chosen[e], weight)
    on = place_of == slot
    pick = jnp.where(on, 1.0, 0.0).astype(BF)
    pick_out[...] = pick
    gate = jnp.sum(jnp.where(on, weight, 0.0), axis=1, keepdims=True)
    for q in range(N):
        for copy in copies[q * 4 : q * 4 + 4]:
            copy.wait()
        for c in range(2):
            cols = slice(c * HALF + q * EIGHTH, c * HALF + (q + 1) * EIGHTH)
            rows = mm(pick, tok_buf[:, cols], NN)
            scaled = mm(pick, grad_buf[:, cols], NN) * gate
            for e in range(N):
                at = slice(e * SLOT, (e + 1) * SLOT)
                both = jnp.concatenate([rows[at], scaled[at]], axis=0).astype(BF)
                out[e * N + q, :, c * EIGHTH : (c + 1) * EIGHTH] = both


def route(ids, gates, tokens, grad_out):
    tok = tokens.shape[0]
    vmem = pl.BlockSpec(memory_space=pltpu.VMEM)
    hbm = pl.BlockSpec(memory_space=pltpu.HBM)
    return pl.pallas_call(
        route_kernel,
        name="route",
        in_specs=[hbm] * 4,
        out_specs=[vmem, vmem],
        out_shape=[
            jax.ShapeDtypeStruct((N * N, 2 * SLOT, QUARTER), BF),
            jax.ShapeDtypeStruct((ROWS, tok), BF),
        ],
        scratch_shapes=[
            pltpu.VMEM(ids.shape, jnp.int32),
            pltpu.VMEM(gates.shape, F32),
            pltpu.VMEM((tok, D), BF),
            pltpu.VMEM((tok, D), BF),
            pltpu.SemaphoreType.DMA((4 * N + 2,)),
        ],
        cost_estimate=pl.CostEstimate(
            flops=4 * ROWS * tok * D, bytes_accessed=6 * tok * D, transcendentals=0
        ),
        compiler_params=pltpu.CompilerParams(vmem_limit_bytes=VMEM_MOST),
    )(ids, gates, tokens, grad_out)


def pair_kernel(place, got, a, b):
    for g in range(N):
        pieces = [got[x * N + g].astype(F32) for x in range(N)]
        for part in range(2):
            rows = [v[part * SLOT : (part + 1) * SLOT] for v in pieces]
            at = (part * 2 + g % 2) * ROWS
            (a, b)[g // 2][at : at + ROWS] = jnp.concatenate(rows, axis=0).astype(BF)


def stack_kernel(place, a0, b0, a1, b3, plus, minus):
    plus[:GROUPED] = a1[...]
    plus[GROUPED:] = b0[...]
    minus[:GROUPED] = b3[...]
    minus[GROUPED:] = a0[...]


def pieces_of(refs):
    if len(refs) == 4:
        a, b, c, d = refs
        return a, b, c, d
    plus, minus = refs
    low, high = pl.ds(0, GROUPED), pl.ds(GROUPED, GROUPED)
    return plus.at[low], minus.at[low], minus.at[high], plus.at[high]


def stack_weights_kernel(place, *refs):
    *pieces, own, other = refs
    y = place[2]
    for out, parts in ((own, pieces[:N]), (other, pieces[N:])):
        for k, w in enumerate(parts):
            block = wrap(y - k)
            for part in range(3):
                rows = pl.ds(pl.multiple_of(part * N * HID + block * HID, HID), HID)
                out[rows, :] = w[part * HID : (part + 1) * HID]


def split_columns_kernel(place, w, o0, o1, o2, o3):
    y = place[2]
    for k, o in enumerate((o0, o1, o2, o3)):
        o[...] = w[0, :, pl.ds(aligned(wrap(y + k) * EIGHTH), EIGHTH)]


def forward_kernel(place, *refs):
    *chunk, own, other, o0, o1, o2, o3, part = refs
    pieces = pieces_of(chunk)
    y, c = place[2], place[3]
    width = N * HID
    mine = pl.ds(aligned(c * EIGHTH), EIGHTH)
    theirs = pl.ds(aligned((1 - c) * EIGHTH), EIGHTH)
    for rows, span in (
        (slice(0, HELD), slice(0, 2 * width)),
        (slice(HELD, 2 * HELD), slice(2 * width, 3 * width)),
    ):
        v_mine = jnp.concatenate([v[rows, mine] for v in pieces], axis=0)
        v_theirs = jnp.concatenate([v[rows, theirs] for v in pieces], axis=0)
        part[:, span] = mm(v_mine, own[span], NT) + mm(v_theirs, other[span], NT)
    for k, o in enumerate((o0, o1, o2, o3)):
        at = wrap(y - k) * ROWS
        for s in range(2):
            rows = pl.ds(pl.multiple_of(s * GROUPED + at, ROWS), ROWS)
            o[s * ROWS : (s + 1) * ROWS] = part[rows, :].astype(o.dtype)


def middle_kernel(place, p0, p1, p2, p3, out):
    width = N * HID
    total = p0[...] + p1[...].astype(F32) + p2[...].astype(F32) + p3[...].astype(F32)
    pair = total[:, : 2 * width]
    d_hidden = total[:, 2 * width :]
    gate = pair[:, :width]
    up = pair[:, width:]
    sig = jax.nn.sigmoid(gate)
    act = gate * sig
    out[:, :width] = (d_hidden * up * sig * (1.0 + gate * (1.0 - sig))).astype(BF)
    out[:, width : 2 * width] = (d_hidden * act).astype(BF)
    out[:, 2 * width :] = (act * up).astype(BF)


def back_kernel(place, held, own, other, *outs):
    c = place[3]
    width = 2 * N * HID
    h = held[:, :width]
    if len(outs) == 2:
        minus, plus = outs
        targets = (minus, 0), (plus, 0), (plus, HELD), (minus, HELD)
    else:
        targets = [(o, 0) for o in outs]
    for w, half in ((own, c), (other, 1 - c)):
        cols = pl.ds(aligned(half * EIGHTH), EIGHTH)
        part = mm(h, w[:width], NN)
        for i, (o, at) in enumerate(targets):
            o[at : at + HELD, cols] = part[i * HELD : (i + 1) * HELD].astype(BF)


def pass_on_kernel(place, own_a, own_b, got_a, got_b, out_a, out_b):
    out_a[...] = (own_a[...].astype(F32) + got_a[:HELD].astype(F32)).astype(BF)
    out_b[...] = (own_b[...].astype(F32) + got_b[:HELD].astype(F32)).astype(BF)


def weight_grad(half, held, chunk, add):
    pieces = pieces_of(chunk)
    width = 2 * N * HID
    cols = pl.ds(aligned(half * EIGHTH), EIGHTH)
    x = jnp.concatenate([v[:HELD, cols] for v in pieces], axis=0)
    add(slice(0, width), mm(held[:, :width], x, TN))
    g = jnp.concatenate([v[HELD : 2 * HELD, cols] for v in pieces], axis=0)
    add(slice(width, 3 * N * HID), mm(held[:, width:], g, TN))


def assemble(y, parts, held):
    for k, h in enumerate(parts):
        at = wrap(y - k) * ROWS
        for s in range(2):
            rows = pl.ds(pl.multiple_of(s * GROUPED + at, ROWS), ROWS)
            held[rows, :] = h[s * ROWS : (s + 1) * ROWS]


def first_grad_kernel(place, *refs):
    *chunk, held, theirs, mine = refs[N:]
    assemble(place[2], refs[:N], held)
    for out, half in ((theirs, 1 - place[3]), (mine, place[3])):

        def add(rows, value, out=out):
            out[rows] = value

        weight_grad(half, held, chunk, add)


def their_grad_kernel(place, *refs):
    before, plus, minus, held, out = refs[N:]
    assemble(place[2], refs[:N], held)

    def add(rows, value):
        out[rows] = (value + before[rows]).astype(BF)

    weight_grad(1 - place[3], held, (plus, minus), add)


def my_grad_kernel(place, got, held, before, plus, minus, o0, o1, o2, o3, mine):
    y = place[2]

    def add(rows, value):
        mine[rows] = value + before[rows]

    weight_grad(place[3], held, (plus, minus), add)
    for k, o in enumerate((o0, o1, o2, o3)):
        block = pl.multiple_of(wrap(y - k) * HID, HID)
        for part in range(3):
            rows = pl.ds(pl.multiple_of(part * N * HID + block, HID), HID)
            total = mine[rows, :] + got[rows, :].astype(F32)
            o[part * HID : (part + 1) * HID] = total.astype(o.dtype)


def sum_back_kernel(place, a0, b0, a1, b3, got_minus, got_plus, out):
    for h, (i, j, k) in enumerate(((a0, a1, got_plus), (b0, b3, got_minus))):
        total = i[...].astype(F32) + (j[...].astype(F32) + k[HELD:].astype(F32))
        for s in range(2):
            for x in range(N):
                at = s * ROWS + x * SLOT
                out[x * N + 2 * h + s] = total[at : at + SLOT].astype(BF)


def combine_kernel(place, pick, got, out, sums, sems):
    copies = []
    for q in range(N):
        rows = jnp.concatenate([got[e * N + q].astype(F32) for e in range(N)], axis=0)
        sums[q] = mm(pick[...], rows.astype(BF), TN).astype(BF)
        for c in range(2):
            copy = pltpu.make_async_copy(
                sums.at[q, :, pl.ds(c * EIGHTH, EIGHTH)],
                out.at[:, pl.ds(c * HALF + q * EIGHTH, EIGHTH)],
                sems.at[q * 2 + c],
            )
            copy.start()
            copies.append(copy)
    for copy in copies:
        copy.wait()


def moments_kernel(place, g0, g1, g2, g3, one, two, new_one, new_two):
    step = pl.program_id(0)
    for k, g in enumerate((g0, g1, g2, g3)):

        @pl.when(step == k)
        def _():
            grad = g[...].astype(F32)
            new_one[0] = beta_one * one[0] + (1.0 - beta_one) * grad
            new_two[0] = beta_two * two[0] + (1.0 - beta_two) * grad * grad


def moments(place, grads, one, two):
    rows = one.shape[1]
    piece = pl.BlockSpec((rows, EIGHTH), lambda k, place: (0, 0))
    block = pl.BlockSpec((1, rows, EIGHTH), lambda k, place: (0, 0, lax.rem(place[2] + k, N)))
    return pl.pallas_call(
        moments_kernel,
        name="moments",
        grid_spec=pltpu.PrefetchScalarGridSpec(
            num_scalar_prefetch=1,
            grid=(N,),
            in_specs=[piece] * N + [block] * 2,
            out_specs=[block] * 2,
        ),
        out_shape=[jax.ShapeDtypeStruct(v.shape, v.dtype) for v in (one, two)],
        cost_estimate=pl.CostEstimate(
            flops=6 * one.size, bytes_accessed=17 * one.size, transcendentals=0
        ),
        compiler_params=pltpu.CompilerParams(vmem_limit_bytes=VMEM_MOST),
    )(place, *grads, one, two)


def exchange(value, axes):
    groups = {}
    for index in range(N * N * N):
        at = {"x": index // (N * N), "z": index // N % N, "y": index % N}
        groups.setdefault(tuple(at[a] for a in at if a not in axes), []).append(index)
    return lax.all_to_all(
        value, "expert", 0, 0, axis_index_groups=list(groups.values()), tiled=True
    )


def spread(parts, axis, sign=1):
    moved = {k: turn(parts[k], axis, sign * k) for k in (2, 1, 3)}
    return [parts[0]] + [moved[k] for k in range(1, N)]


def after(values, *earlier):
    return lax.optimization_barrier((values, earlier))[0]


def pass_on(place, *parts):
    half = ((HELD, QUARTER), BF)
    return call(pass_on_kernel, "pass_on", [half] * 2, place, *parts)


def forward_part(place, chunk, w_own, w_other):
    width = 3 * N * HID
    return call(
        forward_kernel,
        "forward",
        [((HELD, width), F32)] + [((HELD, width), BF)] * 3,
        place,
        *chunk,
        w_own,
        w_other,
        flops=2 * CHUNK * QUARTER * width,
        scratch=[pltpu.VMEM((CHUNK, width), F32)],
    )


def middle_part(place, part):
    return call(middle_kernel, "middle", [((HELD, 3 * N * HID), BF)], place, *part)[0]


def back_part(place, held, w_own, w_other, chunk):
    shape = (HELD, QUARTER) if chunk == 0 else (2 * HELD, QUARTER)
    return call(
        back_kernel,
        "back",
        [(shape, BF)] * (CHUNK // shape[0]),
        place,
        held,
        w_own,
        w_other,
        flops=4 * CHUNK * QUARTER * N * HID,
    )


def shards(tokens, grad_out, gates, expert_ids, expert_weights, moment_one, moment_two):
    expert = lax.axis_index("expert")
    core = lax.axis_index("dp")
    place = jnp.stack([expert // (N * N), expert // N % N, expert % N, core]).astype(jnp.int32)
    tok = tokens.shape[0]
    width = N * HID
    slots = ((N * N, SLOT, QUARTER), BF)
    block_rows = expert_weights.shape[1]

    sent, pick = route(expert_ids.T, gates.T, tokens, grad_out)
    got = exchange(sent, "xy")
    w_columns = call(
        split_columns_kernel,
        "split_columns",
        [((block_rows, EIGHTH), BF)] * N,
        place,
        expert_weights,
    )
    w_parts = spread(w_columns, "y")
    got = after(got, w_columns[1])
    a0, b0 = call(pair_kernel, "pair", [((GROUPED, QUARTER), BF)] * 2, place, got)
    a1, b3 = turn(a0, "z", 1), turn(b0, "z", -1)
    first = a0, b0, a1, b3
    plus, minus = call(
        stack_kernel, "stack", [((2 * GROUPED, QUARTER), BF)] * 2, place, *first
    )
    w_parts = after(w_parts, plus)
    second = turn(plus, "z", 1), turn(minus, "z", -1)
    w_others = [turn(w, "c", 1) for w in w_parts]
    w_own, w_other = call(
        stack_weights_kernel,
        "stack_weights",
        [((N * block_rows, EIGHTH), BF)] * 2,
        place,
        *w_parts,
        *w_others,
    )

    part_one = forward_part(place, first, w_own, w_other)
    part_one = spread(part_one, "y", -1)
    part_two = forward_part(place, second, w_own, w_other)
    part_one = after(part_one, part_two[1])
    part_two = spread(part_two, "y", -1)
    mid_one = middle_part(place, part_one)
    held_one = spread([mid_one] * N, "y")
    mid_two = middle_part(place, part_two)
    held_two = spread([mid_two] * N, "y")
    flops = N * GROUPED * QUARTER * 3 * width
    held_one, first_theirs, first_mine = call(
        first_grad_kernel,
        "first_grad",
        [((CHUNK, 3 * width), BF)] + [((3 * width, EIGHTH), F32)] * 2,
        place,
        *held_one,
        *first,
        flops=flops,
    )
    a0, b0, a1, b3 = back_part(place, held_one, w_own, w_other, 0)
    held_two = after(held_two, a0)
    held_two, theirs = call(
        their_grad_kernel,
        "their_grad",
        [((CHUNK, 3 * width), BF), ((3 * width, EIGHTH), BF)],
        place,
        *held_two,
        first_theirs,
        *second,
        flops=flops // 2,
    )
    minus, plus = back_part(place, held_two, w_own, w_other, 1)
    got_minus, got_plus = turn(minus, "z", -1), turn(plus, "z", 1)
    got = turn(theirs, "c", 1)
    blocks = call(
        my_grad_kernel,
        "my_grad",
        [((block_rows, EIGHTH), F32)] + [((block_rows, EIGHTH), BF)] * 3,
        place,
        got,
        after(held_two, minus),
        first_mine,
        *second,
        flops=flops // 2,
        scratch=[pltpu.VMEM((3 * width, EIGHTH), F32)],
    )
    a1, b3 = pass_on(place, *after((a1, b3, got_minus, got_plus), blocks[0]))
    a1, b3 = turn(a1, "z", -1), turn(b3, "z", 1)
    blocks = spread(blocks, "y", -1)
    parts = after((a0, b0, a1, b3, got_minus, got_plus), *blocks)
    (back,) = call(sum_back_kernel, "sum_back", [slots], place, *parts)
    back = exchange(back, "xy")
    new_one, new_two = moments(place, blocks, moment_one, moment_two)
    back = after(back, new_one)
    (grad_tokens,) = call(
        combine_kernel,
        "combine",
        [((tok, D), BF)],
        place,
        pick,
        back,
        flops=2 * ROWS * tok * D,
        scratch=[pltpu.VMEM((N, tok, QUARTER), BF), pltpu.SemaphoreType.DMA((2 * N,))],
        own_copies=(0,),
    )
    return grad_tokens, new_one, new_two


def solution(mesh):
    return jax.shard_map(
        shards,
        mesh=mesh,
        in_specs=(
            P(("expert", "dp"), None),
            P(("expert", "dp"), None),
            P(("expert", "dp"), None),
            P(("expert", "dp"), None),
            P("expert", None, "dp"),
            P("expert", None, "dp"),
            P("expert", None, "dp"),
        ),
        out_specs=(P(("expert", "dp"), None), P("expert", None, "dp"), P("expert", None, "dp")),
        check_vma=False,
    )
```
